32 devices in a mesh: gx: 4 (over z), gy: 4 (over y, x), layer: 2 (over core).
Axes of the slice: x: 2, y: 2, z: 4, core: 2. Of those that a mesh axis runs over, the one named last changes fastest.
Arguments:
- load_current: float32 [8, 64, 2048], P('layer', 'gx', 'gy'), may hold values from -12 to 12
- pad_cond: float32 [8, 64, 2048], P('layer', 'gx', 'gy'), may hold values from 0.01 to 0.1
- cond_x: float32 [8, 64, 2048], P('layer', 'gx', 'gy'), may hold values from 0.5 to 4
- cond_y: float32 [8, 64, 2048], P('layer', 'gx', 'gy'), may hold values from 0.5 to 4
- via_map: int32 [8, 64, 2048], P('layer', 'gx', 'gy'), may hold values from 0 to 3
- branch_index: int32 [4096, 256], P(('gx', 'gy', 'layer')), may hold values from 0 to 7679
- tree_owner: int32 [4096, 1], P(('gx', 'gy', 'layer')), may hold values from 0 to 15; in each aligned block of 128 rows (0 to 127, 128 to 255, ...) at most 16 rows name the same one
- initial_stress: float32 [4096, 256], P(('gx', 'gy', 'layer')), may hold values from -6 to 6
- block_inverse: float32 [16, 256, 256], P(('gx', 'gy')), may hold values from -1.5 to 1.5
Outputs:
- drop: float32 [8, 64, 2048], P('layer', 'gx', 'gy')
- final_stress: float32 [4096, 256], P(('gx', 'gy', 'layer'))
The draws below stay inside these ranges and needn't reach their ends.
Inputs may be any that keep to these rules, and one draw needn't show every extreme that they name: `tree_owner`: among the 128 trees of one device at most 16 have one owner, and some owner has exactly 16. Owners count in gx+gy order within the tree's own layer group. `branch_index`: A branch joins a node to its next node along x inside the home tile.
All inputs are finite; a program needn't handle non-finite values.
Results may differ from the reference program's by a relative error of at most 0.0003.
Values sent between devices are 32-bit elements; how exact they have to be, the bound alone decides.
A program may use at most 64 MiB of HBM per device.

```python
import math
import jax
import jax.numpy as jnp
import numpy as np
from jax import lax

LPD = 4
CX = 16
CY = 512
KX = 2
KY = 4
ITERS = 2
SWEEPS = 4
STEPS = 8
S = 256
TREES_DEV = 128
L = 8
NX = 64
NY = 2048
NOWN = 16
CAP = 16
TREES = 4096
N_GX = 4
N_GY = 4
N_LAYER = 2


def draw_load_current(key, part):
    key = jax.random.fold_in(key, 11)
    xs = jnp.arange(NX, dtype=jnp.float32) / max(NX - 1, 1)
    rise = (1.0 + 2.0 * xs)[None, :, None]
    return jnp.clip(jax.random.normal(key, (L, NX, NY), jnp.float32), -4.0, 4.0) * rise


def draw_block_inverse(key, part):
    key = jax.random.fold_in(key, 23)
    key_diag, key_off = jax.random.split(key)
    eye = jnp.eye(S, dtype=jnp.float32)
    diag = jax.random.uniform(key_diag, (NOWN, S), jnp.float32, 0.5, 0.8)
    scale = 0.3 / S ** 0.5
    off = jnp.clip(jax.random.normal(key_off, (NOWN, S, S), jnp.float32), -4.0, 4.0)
    return diag[:, :, None] * eye[None] + scale * off * (1.0 - eye[None])


def touch_ends(entries, rng, least, high):
    longest = entries.shape.index(max(entries.shape))
    spots = []
    for shift in (0, 1):
        where = [jax.random.randint(jax.random.fold_in(rng, axis), (), 0, length) for axis, length in enumerate(entries.shape)]
        where[longest] = (where[longest] + shift) % entries.shape[longest]
        spots.append(tuple(where))
    return entries.at[spots[0]].set(least).at[spots[1]].set(high)


def steps_of(own_key, extent, cuts, low, top_value):
    def one(position, shards_of):
        steps = jax.random.uniform(jax.random.fold_in(jax.random.fold_in(own_key, 6), position), (shards_of,), jnp.float32, low / len(cuts), top_value / len(cuts))
        return jnp.repeat(jnp.exp(steps), extent[position] // shards_of).reshape((-1,) + (1,) * (len(extent) - position - 1))

    level = one(*cuts[0])
    for cut in cuts[1:]:
        level = level * one(*cut)
    return level


def assign_block(key, own, number, rows, count, top, bound, lean):
    sequence = jax.random.permutation(key, count)
    crowded, common = load_shares(count, rows * top, bound, lean, True), load_shares(count, rows * top, bound, lean, False)
    places = jnp.arange(count)

    def named(tallies, rotation):
        used = int((tallies > 0).sum())
        fixed = max(1, used // 4)
        moved = fixed + (places - fixed + rotation * (used - fixed)) % max(1, count - fixed)
        return jnp.zeros((count,), jnp.int32).at[sequence[jnp.where(places < fixed, places, moved)]].set(jnp.asarray(tallies, jnp.int32))

    tallies = jnp.where(number % 4 == 0, named(crowded, number // 4), named(common, number - number // 4 - 1))
    mixed = jax.random.permutation(jax.random.fold_in(own, 3), count)
    giver, receiver = mixed[0:count // 2 * 2:2], mixed[1:count // 2 * 2:2]
    slack = jnp.minimum(tallies[giver] - 1, bound - tallies[receiver]) // 2
    slack = jnp.where((giver == sequence[0]) | (receiver == sequence[0]) | (tallies[receiver] == 0), 0, jnp.maximum(slack, 0))
    moved = jax.random.randint(jax.random.fold_in(own, 4), (count // 2,), 0, 1 << 20) % (slack + 1)
    tallies = tallies.at[giver].add(-moved).at[receiver].add(moved)
    members = jnp.searchsorted(jnp.cumsum(tallies), jnp.arange(rows * top), side="right").astype(jnp.int32)
    table = members.reshape(top, rows).T
    table = table[jax.random.permutation(jax.random.fold_in(own, 1), rows)]
    rotation = jax.random.randint(jax.random.fold_in(own, 2), (rows, 1), 0, top)
    return jnp.take_along_axis(table, (jnp.arange(top)[None, :] + rotation) % top, axis=1)


def load_shares(number_of, total, bound, lean, full):
    portions = [(1 << 20) // math.isqrt(grade ** lean) + 1 for grade in range(1, number_of + 1)]
    largest = bound if full else min(bound, max(-(-total // number_of), total * portions[0] // sum(portions)))
    least = 1 if total - largest >= number_of - 1 else 0
    holding, rest = [largest] + [least] * (number_of - 1), total - largest - least * (number_of - 1)
    while rest > 0:
        movable = [i for i in range(1, number_of) if holding[i] < largest] or [i for i in range(1, number_of) if holding[i] < bound]
        mass, budget = sum([portions[i] for i in movable]), rest
        for i in movable:
            extra = min(bound - holding[i], max(1, budget * portions[i] // mass), rest)
            holding[i] = holding[i] + extra
            rest = rest - extra
    return np.array(holding)


def scatter_about(stream_key, dims, scale, bound, cuts=(), kind=jnp.bfloat16):
    array = scale * jax.random.normal(stream_key, dims, jnp.float32)
    if cuts:
        array = array * steps_of(stream_key, dims, cuts, -0.22, 0.18)
    return jnp.clip(array, -bound, bound).astype(kind)


def setup_inputs(seed: int = 0) -> dict:
    streams_of = jax.random.split(jax.random.key(seed), 10)
    load_current = draw_load_current(jax.random.fold_in(streams_of[9], 71), 0)
    pad_cond = jnp.clip(jnp.exp(math.log(0.1) - 2.3025851 * jax.random.uniform(streams_of[1], (L, NX, NY), jnp.float32) ** steps_of(streams_of[1], (L, NX, NY), ((0, 2), (1, 4), (2, 4)), -0.2, 0.2)), 0.01, 0.1)
    cond_x = jnp.clip(jnp.exp(math.log(4.0) - 2.0794415 * jax.random.uniform(streams_of[2], (L, NX, NY), jnp.float32) ** steps_of(streams_of[2], (L, NX, NY), ((0, 2), (1, 4), (2, 4)), -0.2, 0.2)), 0.5, 4.0)
    cond_y = jnp.clip(jnp.exp(math.log(4.0) - 2.0794415 * jax.random.uniform(streams_of[3], (L, NX, NY), jnp.float32) ** steps_of(streams_of[3], (L, NX, NY), ((0, 2), (1, 4), (2, 4)), -0.2, 0.2)), 0.5, 4.0)
    via_map = touch_ends(jax.random.randint(streams_of[4], (L, NX, NY), 0, 4), jax.random.fold_in(streams_of[4], 1), 0, 3).astype(jnp.int32)
    branch_index = touch_ends(jax.random.randint(streams_of[5], (TREES, S), 0, (CX - 1) * CY), jax.random.fold_in(streams_of[5], 1), 0, ((CX - 1) * CY) - 1).astype(jnp.int32)
    tree_owner_keys = jax.random.split(jax.random.fold_in(streams_of[6], 1), TREES // TREES_DEV)
    tree_owner_turns = jax.random.permutation(jax.random.fold_in(streams_of[6], 3), TREES // TREES_DEV)
    tree_owner = jax.vmap(lambda own, number: assign_block(jax.random.fold_in(streams_of[6], 2), own, number, TREES_DEV, N_GX * N_GY, 1, CAP, 2))(tree_owner_keys, tree_owner_turns).reshape((TREES, 1))
    initial_stress = scatter_about(streams_of[7], (TREES, S), 1.0, 6.0, ((0, 32),), jnp.float32)
    block_inverse = draw_block_inverse(jax.random.fold_in(streams_of[9], 71), 0)
    return dict(load_current=load_current, pad_cond=pad_cond, cond_x=cond_x, cond_y=cond_y, via_map=via_map, branch_index=branch_index, tree_owner=tree_owner, initial_stress=initial_stress, block_inverse=block_inverse)


OMEGA = 0.7
TAU = 0.6
VIA_G = 1.5
COARSE_G = 64.0
KAPPA = 2.0


def link_fields(cond_x, cond_y, via_map):
    mask_x = (jnp.arange(NX) < NX - 1).astype(jnp.float32)
    mask_y = (jnp.arange(NY) < NY - 1).astype(jnp.float32)
    mask_z = (jnp.arange(L) < L - 1).astype(jnp.float32)
    link_x = cond_x * mask_x[None, :, None]
    link_y = cond_y * mask_y[None, None, :]
    link_z = via_map.astype(jnp.float32) * VIA_G * mask_z[:, None, None]
    return link_x, link_y, link_z


def operate(field, pads, links):
    link_x, link_y, link_z = links
    padded = jnp.pad(field, 1)
    pad_x = jnp.pad(link_x, 1)
    pad_y = jnp.pad(link_y, 1)
    pad_z = jnp.pad(link_z, 1)
    out = pads * field
    out = out + link_x * (field - padded[1:-1, 2:, 1:-1]) + pad_x[1:-1, :-2, 1:-1] * (field - padded[1:-1, :-2, 1:-1])
    out = out + link_y * (field - padded[1:-1, 1:-1, 2:]) + pad_y[1:-1, 1:-1, :-2] * (field - padded[1:-1, 1:-1, :-2])
    out = out + link_z * (field - padded[2:, 1:-1, 1:-1]) + pad_z[:-2, 1:-1, 1:-1] * (field - padded[:-2, 1:-1, 1:-1])
    return out


def diagonal_of(pads, links):
    link_x, link_y, link_z = links
    pad_x = jnp.pad(link_x, 1)
    pad_y = jnp.pad(link_y, 1)
    pad_z = jnp.pad(link_z, 1)
    total = pads + link_x + pad_x[1:-1, :-2, 1:-1]
    total = total + link_y + pad_y[1:-1, 1:-1, :-2]
    return total + link_z + pad_z[:-2, 1:-1, 1:-1]


def restrict(field):
    shaped = field.reshape(N_LAYER, LPD, KX * N_GX, CX // KX, KY * N_GY, CY // KY)
    return jnp.sum(shaped, axis=(1, 3, 5))


def prolong(coarse):
    spread = jnp.broadcast_to(coarse[:, None, :, None, :, None], (N_LAYER, LPD, KX * N_GX, CX // KX, KY * N_GY, CY // KY))
    return spread.reshape(L, NX, NY)


def coarse_solve(coarse_rhs, cdiag):
    diag = cdiag + 6.0 * COARSE_G
    value = jnp.zeros_like(coarse_rhs)
    for sweep in range(SWEEPS):
        padded = jnp.pad(value, 1)
        beside_all = padded[:-2, 1:-1, 1:-1] + padded[2:, 1:-1, 1:-1]
        beside_all = beside_all + padded[1:-1, 2:, 1:-1] + padded[1:-1, :-2, 1:-1]
        beside_all = beside_all + padded[1:-1, 1:-1, 2:] + padded[1:-1, 1:-1, :-2]
        value = value + TAU * (coarse_rhs - (diag * value - COARSE_G * beside_all)) / diag
    return value


def reference(load_current, pad_cond, cond_x, cond_y, via_map, branch_index, tree_owner, initial_stress, block_inverse):
    links = link_fields(cond_x, cond_y, via_map)
    diag = diagonal_of(pad_cond, links)
    cdiag = restrict(pad_cond)

    def precondition(resid):
        return OMEGA * resid / diag + prolong(coarse_solve(restrict(resid), cdiag))

    drop = jnp.zeros_like(load_current)
    resid = load_current
    zvec = precondition(resid)
    direction = zvec
    rz_now = jnp.sum(resid * zvec)
    for step in range(ITERS):
        image = operate(direction, pad_cond, links)
        alpha = rz_now / jnp.sum(direction * image)
        drop = drop + alpha * direction
        resid = resid - alpha * image
        zvec = precondition(resid)
        rz_next = jnp.sum(resid * zvec)
        direction = zvec + (rz_next / rz_now) * direction
        rz_now = rz_next

    link_x = links[0]
    trees = jnp.arange(TREES, dtype=jnp.int32)
    home = trees // TREES_DEV
    home_x = home // (N_GY * N_LAYER)
    home_y = (home // N_LAYER) % N_GY
    home_l = home % N_LAYER
    lyr = (jnp.arange(S, dtype=jnp.int32) % LPD)[None, :]
    row = branch_index // CY
    col = branch_index % CY
    glob_l = home_l[:, None] * LPD + lyr
    glob_i = home_x[:, None] * CX + row
    glob_j = home_y[:, None] * CY + col
    current = link_x[glob_l, glob_i, glob_j] * (drop[glob_l, glob_i, glob_j] - drop[glob_l, glob_i + 1, glob_j])

    blocks = TREES // TREES_DEV
    cur_b = current.reshape(blocks, TREES_DEV, S)
    stress_b = initial_stress.reshape(blocks, TREES_DEV, S)
    owner_b = tree_owner[:, 0].reshape(blocks, TREES_DEV)

    def one_block(items):
        flow, stress, owners = items
        mats = block_inverse[owners]
        for step in range(STEPS):
            stress = jnp.einsum("bus,bs->bu", mats, stress + KAPPA * flow, precision=lax.Precision.HIGHEST)
        return stress

    final_stress = lax.map(one_block, (cur_b, stress_b, owner_b)).reshape(TREES, S)
    return drop, final_stress
```

```python
import functools

import jax
import jax.numpy as jnp
from jax import lax
from jax.experimental import pallas as pl
from jax.experimental.pallas import tpu as pltpu
from jax.sharding import PartitionSpec as P

KX = 2
KY = 4
SWEEPS = 4
STEPS = 8

OMEGA = 0.7
TAU = 0.6
VIA_G = 1.5
COARSE_G = 64.0
KAPPA = 2.0
LANES = 128
HALF = 64
MESH = pl.DeviceIdType.MESH


def iota(shape, dim):
    return lax.broadcasted_iota(jnp.int32, shape, dim)


def sum_all(v):
    while v.ndim > 2:
        v = jnp.sum(v, axis=0)
    return jnp.sum(jnp.sum(v, axis=0, keepdims=True), axis=1, keepdims=True)


def cg_kernel(
    sizes,
    load_ref, pad_ref, cx_ref, cy_ref, via_ref,
    drop_ref, flow_ref,
    links, downs, dinv_ref, w_ref, p_ref, q_ref,
    xsend, xrecv, yrecv, zrecv, lxsend, lxrecv, lyrecv, lzrecv,
    tsend, trecv,
    link_send, link_recv, halo_send, halo_recv, tile_send, tile_recv,
):
    sx, sy, sl = sizes
    n = sx * sy * sl
    layers, rows, cols = load_ref.shape
    br, bc = rows // KX, cols // KY
    nyc = KY * sy
    grid_rows = KX * sx
    gx, gy, gl = lax.axis_index("gx"), lax.axis_index("gy"), lax.axis_index("layer")
    me = (gx * sy + gy) * sl + gl

    def coords(flat):
        return (flat // (sy * sl), (flat // sl) % sy, flat % sl)

    barrier = pltpu.get_barrier_semaphore()

    def greet(k, carry):
        pl.semaphore_signal(
            barrier, inc=1, device_id=coords(lax.rem(me + k, n)), device_id_type=MESH
        )
        return carry

    lax.fori_loop(1, n, greet, 0)

    up_dev = (
        (lax.rem(gx + 1, sx), gy, gl),
        (gx, lax.rem(gy + 1, sy), gl),
        (gx, gy, lax.rem(gl + 1, sl)),
    )
    down_dev = (
        (lax.rem(gx + sx - 1, sx), gy, gl),
        (gx, lax.rem(gy + sy - 1, sy), gl),
        (gx, gy, lax.rem(gl + sl - 1, sl)),
    )

    shape = (layers, rows, cols)
    plane_of = iota(shape, 0)
    row_of = iota(shape, 1)
    col_of = iota(shape, 2)
    links[0] = jnp.where(gx * rows + row_of < rows * sx - 1, cx_ref[...], 0.0)
    links[1] = jnp.where(gy * cols + col_of < cols * sy - 1, cy_ref[...], 0.0)
    links[2] = jnp.where(
        gl * layers + plane_of < layers * sl - 1, via_ref[...].astype(jnp.float32) * VIA_G, 0.0
    )
    lxsend[...] = links[0, :, rows - 1 : rows, :]

    tile_shape = (grid_rows, LANES)
    trow = iota(tile_shape, 0)
    tlane = iota(tile_shape, 1)
    lane0 = gl * nyc + gy * KY
    valid = tlane < sl * nyc

    def restrict_into(tile, field, shift):
        flat = jnp.sum(field, axis=0)
        for a in range(KX):
            for b in range(KY):
                val = sum_all(flat[a * br : (a + 1) * br, b * bc : (b + 1) * bc])
                here = (trow == gx * KX + a) & (tlane == lane0 + b + shift)
                tile = jnp.where(here, val, tile)
        return tile

    def send_tile(phase):
        def one(k, carry):
            pltpu.make_async_remote_copy(
                src_ref=tsend.at[phase],
                dst_ref=trecv.at[phase, k - 1],
                send_sem=tile_send.at[phase],
                recv_sem=tile_recv.at[phase],
                device_id=coords(lax.rem(me + k, n)),
                device_id_type=MESH,
            ).start()
            return carry

        lax.fori_loop(1, n, one, 0)

    def wait_tile(phase):
        every = trecv.at[phase]
        pltpu.make_async_copy(every, every, tile_recv.at[phase]).wait()
        return jnp.sum(trecv[phase], axis=0) + tsend[phase]

    def drain_tile(phase):
        every = trecv.at[phase]
        pltpu.make_async_copy(every, every, tile_send.at[phase]).wait()

    tile = jnp.zeros(tile_shape, jnp.float32)
    tile = restrict_into(tile, load_ref[...], 0)
    tsend[0] = restrict_into(tile, pad_ref[...], HALF)

    def remote(src, dst, send, recv, device):
        return pltpu.make_async_remote_copy(
            src_ref=src, dst_ref=dst, send_sem=send, recv_sem=recv,
            device_id=device, device_id_type=MESH,
        )

    last = pl.ds(cols - LANES, LANES)
    link_copies = [
        remote(lxsend, lxrecv, link_send.at[0], link_recv.at[0], up_dev[0]),
        remote(links.at[1, :, :, last], lyrecv, link_send.at[1], link_recv.at[1], up_dev[1]),
        remote(links.at[2, layers - 1], lzrecv, link_send.at[2], link_recv.at[2], up_dev[2]),
    ]

    def halo_copies(h):
        pairs = [
            (xsend.at[h, 0], xrecv.at[h, 0], up_dev[0]),
            (xsend.at[h, 1], xrecv.at[h, 1], down_dev[0]),
            (w_ref.at[h, :, :, last], yrecv.at[h, 0], up_dev[1]),
            (w_ref.at[h, :, :, pl.ds(0, LANES)], yrecv.at[h, 1], down_dev[1]),
            (w_ref.at[h, layers - 1], zrecv.at[h, 0], up_dev[2]),
            (w_ref.at[h, 0], zrecv.at[h, 1], down_dev[2]),
        ]
        return [
            remote(src, dst, halo_send.at[h, i], halo_recv.at[h, i], dev)
            for i, (src, dst, dev) in enumerate(pairs)
        ]

    def from_below(v, x_lo, y_lo, z_lo):
        vx = jnp.where(row_of == 0, x_lo, pltpu.roll(v, 1, 1))
        edge = jnp.concatenate([pltpu.roll(y_lo, 1, 2), v[:, :, LANES:]], axis=2)
        vy = jnp.where(col_of == 0, edge, pltpu.roll(v, 1, 2))
        vz = jnp.concatenate([z_lo[None], v[:-1]], axis=0)
        return vx, vy, vz

    def from_above(v, x_hi, y_hi, z_hi):
        vx = jnp.where(row_of == rows - 1, x_hi, pltpu.roll(v, rows - 1, 1))
        edge = jnp.concatenate([v[:, :, :-LANES], pltpu.roll(y_hi, LANES - 1, 2)], axis=2)
        vy = jnp.where(col_of == cols - 1, edge, pltpu.roll(v, cols - 1, 2))
        vz = jnp.concatenate([v[1:], z_hi[None]], axis=0)
        return vx, vy, vz

    pl.semaphore_wait(barrier, n - 1)
    for copy in link_copies:
        copy.start()
    send_tile(0)

    for copy in link_copies:
        copy.wait()
    down_x, _, _ = from_below(links[0], lxrecv[...], lyrecv[...], lzrecv[...])
    _, down_y, _ = from_below(links[1], lxrecv[...], lyrecv[...], lzrecv[...])
    _, _, down_z = from_below(links[2], lxrecv[...], lyrecv[...], lzrecv[...])
    downs[0] = down_x
    downs[1] = down_y
    downs[2] = down_z
    diag = pad_ref[...] + links[0] + down_x + links[1] + down_y + links[2] + down_z
    dinv = OMEGA / diag
    dinv_ref[...] = dinv
    w0 = load_ref[...] * dinv

    def put_halo(h, w):
        w_ref[h] = w
        xsend[h, 0] = w[:, rows - 1 : rows, :]
        xsend[h, 1] = w[:, 0:1, :]

    put_halo(0, w0)
    first = halo_copies(0)
    for copy in first:
        copy.start()

    total0 = wait_tile(0)
    c0 = jnp.where(valid, total0, 0.0)
    cfull = jnp.where(valid, pltpu.roll(total0, LANES - HALF, 1), 0.0) + 6.0 * COARSE_G
    in_layer = lax.rem(tlane, nyc)

    def coarse(c):
        y = TAU * c / cfull
        for _ in range(SWEEPS - 1):
            near = jnp.where(trow > 0, pltpu.roll(y, 1, 0), 0.0)
            near += jnp.where(trow < grid_rows - 1, pltpu.roll(y, grid_rows - 1, 0), 0.0)
            near += jnp.where(in_layer > 0, pltpu.roll(y, 1, 1), 0.0)
            near += jnp.where(in_layer < nyc - 1, pltpu.roll(y, LANES - 1, 1), 0.0)
            near += jnp.where(tlane >= nyc, pltpu.roll(y, nyc, 1), 0.0)
            near += jnp.where(tlane < (sl - 1) * nyc, pltpu.roll(y, LANES - nyc, 1), 0.0)
            y = y + TAU * (c - (cfull * y - COARSE_G * near)) / cfull
            y = jnp.where(valid, y, 0.0)
        return y

    def spread(y):
        t = pltpu.roll(y, lax.rem(grid_rows + 1 - gx * KX, grid_rows), 0)
        t = pltpu.roll(t, lax.rem(LANES + 1 - lane0, LANES), 1)

        def bcast(src, r, c, height):
            return jnp.broadcast_to(src[r : r + 1, c : c + 1], (height, bc))

        def across(src, r, height):
            return jnp.concatenate([bcast(src, r, 1 + b, height) for b in range(KY)], axis=1)

        def whole(src):
            return jnp.concatenate([across(src, 1 + a, br) for a in range(KX)], axis=0)

        def side(c):
            parts = [
                jnp.broadcast_to(t[1 + a : 2 + a, c : c + 1], (br, LANES)) for a in range(KX)
            ]
            return jnp.concatenate(parts, axis=0)

        above = pltpu.roll(t, LANES - nyc, 1)
        below = pltpu.roll(t, nyc, 1)
        return (
            whole(t),
            (across(t, 0, 1), across(t, KX + 1, 1)),
            (side(0), side(KY + 1)),
            (whole(below), whole(above)),
        )

    def operate(v, lows, highs):
        bx, by, bz = from_below(v, *lows)
        ax, ay, az = from_above(v, *highs)
        out = pad_ref[...] * v
        out = out + links[0] * (v - ax) + downs[0] * (v - bx)
        out = out + links[1] * (v - ay) + downs[1] * (v - by)
        return out + links[2] * (v - az) + downs[2] * (v - bz)

    y0 = coarse(c0)
    own0, x0, yy0, z0 = spread(y0)
    coarse_dot0 = sum_all(c0 * y0)
    p0 = w0 + own0[None]
    p_ref[...] = p0
    for copy in first:
        copy.wait()

    lows0 = (xrecv[0, 0] + x0[0][None], yrecv[0, 0] + yy0[0][None], zrecv[0, 0] + z0[0])
    highs0 = (xrecv[0, 1] + x0[1][None], yrecv[0, 1] + yy0[1][None], zrecv[0, 1] + z0[1])
    q0 = operate(p0, lows0, highs0)
    wq = q0 * dinv_ref[...]
    put_halo(1, wq)
    second = halo_copies(1)
    for copy in second:
        copy.start()

    r0 = load_ref[...]
    tile = restrict_into(jnp.zeros(tile_shape, jnp.float32), q0, 0)
    sums = (sum_all(p0 * q0), sum_all(r0 * w_ref[0]), sum_all(r0 * wq), sum_all(q0 * wq))
    for i, val in enumerate(sums):
        tile = jnp.where((trow == 0) & (tlane == HALF + i), val, tile)
    tsend[1] = tile
    send_tile(1)
    total1 = wait_tile(1)

    pq0, rr, rq, qq = (total1[0:1, HALF + i : HALF + i + 1] for i in range(4))
    rz0 = rr + coarse_dot0
    alpha0 = rz0 / pq0
    c1 = jnp.where(valid, c0 - alpha0 * total1, 0.0)
    y1 = coarse(c1)
    rz1 = rr - 2.0 * alpha0 * rq + alpha0 * alpha0 * qq + sum_all(c1 * y1)
    beta = rz1 / rz0
    own1, x1, yy1, z1 = spread(y1)

    p1 = w_ref[0] - alpha0 * w_ref[1] + own1[None] + beta * p_ref[...]
    for copy in second:
        copy.wait()

    def next_halo(first_w, second_w, first_y, second_y):
        return first_w - alpha0 * second_w + second_y + beta * (first_w + first_y)

    lows1, highs1 = (
        (
            next_halo(xrecv[0, s], xrecv[1, s], x0[s][None], x1[s][None]),
            next_halo(yrecv[0, s], yrecv[1, s], yy0[s][None], yy1[s][None]),
            next_halo(zrecv[0, s], zrecv[1, s], z0[s], z1[s]),
        )
        for s in range(2)
    )
    q1 = operate(p1, lows1, highs1)
    tsend[2] = jnp.where((trow == 0) & (tlane == 0), sum_all(p1 * q1), 0.0)
    send_tile(2)
    q_ref[...] = p1
    drain_tile(0)
    drain_tile(1)
    total2 = wait_tile(2)
    alpha1 = rz1 / total2[0:1, 0:1]
    drop = alpha0 * p_ref[...] + alpha1 * q_ref[...]
    drop_ref[...] = drop
    flow_ref[...] = links[0] * (drop - pltpu.roll(drop, rows - 1, 1))
    drain_tile(2)


def run_cg(sizes, load_current, pad_cond, cond_x, cond_y, via_map):
    sx, sy, sl = sizes
    n = sx * sy * sl
    layers, rows, cols = load_current.shape
    field = (layers, rows, cols)
    f32 = jnp.float32
    vmem = pltpu.VMEM
    dma = pltpu.SemaphoreType.DMA
    spec = pl.BlockSpec(memory_space=pltpu.VMEM)
    return pl.pallas_call(
        functools.partial(cg_kernel, sizes),
        out_shape=(jax.ShapeDtypeStruct(field, f32), jax.ShapeDtypeStruct(field, f32)),
        in_specs=[spec] * 5,
        out_specs=(spec, spec),
        scratch_shapes=[
            vmem((3,) + field, f32),
            vmem((3,) + field, f32),
            vmem(field, f32),
            vmem((2,) + field, f32),
            vmem(field, f32),
            vmem(field, f32),
            vmem((2, 2, layers, 1, cols), f32),
            vmem((2, 2, layers, 1, cols), f32),
            vmem((2, 2, layers, rows, LANES), f32),
            vmem((2, 2, rows, cols), f32),
            vmem((layers, 1, cols), f32),
            vmem((layers, 1, cols), f32),
            vmem((layers, rows, LANES), f32),
            vmem((rows, cols), f32),
            vmem((3, KX * sx, LANES), f32),
            vmem((3, n - 1, KX * sx, LANES), f32),
            dma((3,)),
            dma((3,)),
            dma((2, 6)),
            dma((2, 6)),
            dma((3,)),
            dma((3,)),
        ],
        compiler_params=pltpu.CompilerParams(
            collective_id=0, has_side_effects=True, vmem_limit_bytes=48 * 1024 * 1024
        ),
    )(load_current, pad_cond, cond_x, cond_y, via_map)


def gather_kernel(flow_ref, index_ref, out_ref, hi_ref, lo_ref, acc_ref):
    layers, rows, cols = flow_ref.shape
    trees, segs = index_ref.shape
    per = segs // layers
    blocks = cols // LANES
    half = trees // 2
    index = index_ref[...]
    source = iota((segs, segs), 0)
    target = iota((segs, segs), 1)
    sort = (source == (target % per) * layers + target // per).astype(jnp.bfloat16)
    hi = jnp.dot((index // LANES).astype(jnp.bfloat16), sort, preferred_element_type=jnp.float32)
    lo = jnp.dot((index % LANES).astype(jnp.bfloat16), sort, preferred_element_type=jnp.float32)
    hi = hi.astype(jnp.int32)
    lo = lo.astype(jnp.int32)
    left = iota((half, LANES), 1) < per

    def pack(v, l):
        base = (l // 2) * LANES
        top, low = v[:half, base : base + LANES], v[half:, base : base + LANES]
        if l % 2 == 0:
            return jnp.where(left, top, pltpu.roll(low, per, 1))
        return jnp.where(left, pltpu.roll(top, per, 1), low)

    for l in range(layers):
        hi_ref[l] = pack(hi, l)
        lo_ref[l] = pack(lo, l)
    for l in range(layers):
        want = hi_ref[l]
        lane = lo_ref[l]

        acc = jnp.zeros((half, LANES), jnp.float32)
        for i in range(rows - 1):
            for b in range(blocks):
                row = flow_ref[l, i : i + 1, b * LANES : (b + 1) * LANES]
                table = jnp.broadcast_to(row, (half, LANES))
                got = jnp.take_along_axis(table, lane, axis=1, mode="promise_in_bounds")
                acc = jnp.where(want == i * blocks + b, got, acc)
        acc_ref[l] = acc
    tops, lows = [], []
    for l in range(0, layers, 2):
        even, odd = acc_ref[l], acc_ref[l + 1]
        tops.append(jnp.where(left, even, pltpu.roll(odd, per, 1)))
        lows.append(jnp.where(left, pltpu.roll(even, per, 1), odd))
    sorted_flow = jnp.concatenate(
        [jnp.concatenate(tops, axis=1), jnp.concatenate(lows, axis=1)], axis=0
    )
    back = (target == (source % per) * layers + source // per).astype(jnp.float32)
    out_ref[...] = jnp.dot(
        sorted_flow, back, preferred_element_type=jnp.float32, precision=lax.Precision.HIGHEST
    )


def gather_current(flow, branch_index):
    layers = flow.shape[0]
    trees, segs = branch_index.shape
    packed = (layers, trees // 2, LANES)
    spec = pl.BlockSpec(memory_space=pltpu.VMEM)
    return pl.pallas_call(
        gather_kernel,
        out_shape=jax.ShapeDtypeStruct((trees, segs), jnp.float32),
        in_specs=[spec, spec],
        out_specs=spec,
        scratch_shapes=[
            pltpu.VMEM(packed, jnp.int32),
            pltpu.VMEM(packed, jnp.int32),
            pltpu.VMEM(packed, jnp.float32),
        ],
    )(flow, branch_index)


def per_device(
    load_current,
    pad_cond,
    cond_x,
    cond_y,
    via_map,
    branch_index,
    tree_owner,
    initial_stress,
    block_inverse,
):
    size_x = lax.axis_size("gx")
    size_y = lax.axis_size("gy")
    size_l = lax.axis_size("layer")
    drop, field = run_cg(
        (size_x, size_y, size_l), load_current, pad_cond, cond_x, cond_y, via_map
    )
    current = gather_current(field, branch_index)
    trees_dev, segs = initial_stress.shape
    owners_count = size_x * size_y
    capacity = 2 * trees_dev // owners_count
    owners = tree_owner[:, 0]
    hits = (owners[:, None] == jnp.arange(owners_count, dtype=jnp.int32)[None, :]).astype(jnp.int32)
    slot_rank = jnp.sum((jnp.cumsum(hits, axis=0) - hits) * hits, axis=1)
    payload = jnp.stack([current, initial_stress])
    outgoing = (
        jnp.zeros((2, owners_count, capacity, segs), jnp.float32)
        .at[:, owners, slot_rank]
        .set(payload)
    )
    inverse = block_inverse[0]
    piece = lax.all_to_all(outgoing, ("gx", "gy"), split_axis=1, concat_axis=1, tiled=True)
    count = piece.shape[2]
    flow = piece[0].reshape(-1, segs)
    stress = piece[1].reshape(-1, segs)
    for step in range(STEPS):
        stress = jnp.einsum(
            "ts,us->tu", stress + KAPPA * flow, inverse, precision=lax.Precision.HIGHEST
        )
    returning = stress.reshape(owners_count, count, segs)
    solved = lax.all_to_all(returning, ("gx", "gy"), split_axis=0, concat_axis=0, tiled=True)
    final_stress = solved[owners, slot_rank]
    return (drop, final_stress)


def solution(mesh):
    return jax.shard_map(
        per_device,
        mesh=mesh,
        in_specs=(
            P("layer", "gx", "gy"),
            P("layer", "gx", "gy"),
            P("layer", "gx", "gy"),
            P("layer", "gx", "gy"),
            P("layer", "gx", "gy"),
            P(("gx", "gy", "layer"), None),
            P(("gx", "gy", "layer"), None),
            P(("gx", "gy", "layer"), None),
            P(("gx", "gy"), None, None),
        ),
        out_specs=(P("layer", "gx", "gy"), P(("gx", "gy", "layer"), None)),
        check_vma=False,
    )
```

```python
import functools

import jax
import jax.numpy as jnp
from jax import lax
from jax.experimental import pallas as pl
from jax.experimental.pallas import tpu as pltpu
from jax.sharding import PartitionSpec as P

KX = 2
KY = 4
SWEEPS = 4
STEPS = 8

OMEGA = 0.7
TAU = 0.6
VIA_G = 1.5
COARSE_G = 64.0
KAPPA = 2.0
LANES = 128
HALF = 64
MESH = pl.DeviceIdType.MESH


def iota(shape, dim):
    return lax.broadcasted_iota(jnp.int32, shape, dim)


def sum_all(v):
    while v.ndim > 2:
        v = jnp.sum(v, axis=0)
    return jnp.sum(jnp.sum(v, axis=0, keepdims=True), axis=1, keepdims=True)


def cg_kernel(
    sizes,
    capacity,
    load_in, pad_in, cx_in, cy_in, via_in, index_in, stress_in, inverse_in, owner_ref,
    drop_ref, final_ref,
    load_ref, pad_ref, cx_ref, cy_ref, via_ref, index_ref, stress_ref, inverse_ref,
    flow_ref, hi_ref, lo_ref, acc_ref, onehot_ref, base_ref, power_ref,
    ssend, srecv, fsend, frecv, gsend, grecv,
    links, downs, dinv_ref, w_ref, p_ref, q_ref,
    xsend, xrecv, yrecv, zrecv, lxsend, lxrecv, lyrecv, lzrecv,
    tsend, trecv,
    link_send, link_recv, halo_send, halo_recv, tile_send, tile_recv,
    in_sem, tree_send, tree_recv,
):
    sx, sy, sl = sizes
    n = sx * sy * sl
    layers, rows, cols = load_ref.shape
    br, bc = rows // KX, cols // KY
    nyc = KY * sy
    grid_rows = KX * sx
    gx, gy, gl = lax.axis_index("gx"), lax.axis_index("gy"), lax.axis_index("layer")
    me = (gx * sy + gy) * sl + gl

    def coords(flat):
        return (flat // (sy * sl), (flat // sl) % sy, flat % sl)

    loads = [
        pltpu.make_async_copy(src, dst, in_sem.at[i])
        for i, (src, dst) in enumerate((
            (via_in, via_ref), (cx_in, cx_ref), (cy_in, cy_ref), (load_in, load_ref),
            (pad_in, pad_ref), (stress_in, stress_ref), (inverse_in, inverse_ref),
            (index_in, index_ref),
        ))
    ]
    for copy in loads:
        copy.start()
    barrier = pltpu.get_barrier_semaphore()

    def greet(k, carry):
        pl.semaphore_signal(
            barrier, inc=1, device_id=coords(lax.rem(me + k, n)), device_id_type=MESH
        )
        return carry

    lax.fori_loop(1, n, greet, 0)

    up_dev = (
        (lax.rem(gx + 1, sx), gy, gl),
        (gx, lax.rem(gy + 1, sy), gl),
        (gx, gy, lax.rem(gl + 1, sl)),
    )
    down_dev = (
        (lax.rem(gx + sx - 1, sx), gy, gl),
        (gx, lax.rem(gy + sy - 1, sy), gl),
        (gx, gy, lax.rem(gl + sl - 1, sl)),
    )

    np_ = sx * sy
    q = gx * sy + gy
    trees, segs = stress_ref.shape
    slots = np_ * capacity
    high = lax.Precision.HIGHEST

    def exact(a, b):
        return jnp.dot(a, b, preferred_element_type=jnp.float32, precision=high)

    def rows_by(a, b):
        return lax.dot_general(
            a, b, (((1,), (1,)), ((), ())), preferred_element_type=jnp.float32, precision=high
        )

    owner_rel = lax.rem(owner_ref[...] - q + np_, np_)
    hits = owner_rel == iota((trees, LANES), 1)
    ahead = iota((trees, trees), 1) < iota((trees, trees), 0)
    counts = jnp.dot(
        ahead.astype(jnp.bfloat16), hits.astype(jnp.bfloat16), preferred_element_type=jnp.float32
    )
    rank = jnp.sum(jnp.where(hits, counts, 0.0), axis=1, keepdims=True).astype(jnp.int32)
    slot = owner_rel * capacity + rank
    onehot_ref[...] = (slot == iota((trees, slots), 1)).astype(jnp.float32)

    def to_slots(v):
        return lax.dot_general(
            onehot_ref[...], v, (((0,), (0,)), ((), ())),
            preferred_element_type=jnp.float32, precision=high,
        ).reshape(np_, capacity, segs)

    def peer(k):
        flat = lax.rem(q + k, np_)
        return (flat // sy, flat % sy, gl)

    def exchange(phase, src, dst, sign):
        def one(k, carry):
            pltpu.make_async_remote_copy(
                src_ref=src.at[k],
                dst_ref=dst.at[k - 1],
                send_sem=tree_send.at[phase],
                recv_sem=tree_recv.at[phase],
                device_id=peer(k if sign > 0 else np_ - k),
                device_id_type=MESH,
            ).start()
            return carry

        lax.fori_loop(1, np_, one, 0)

    def arrived(phase, dst):
        pltpu.make_async_copy(dst, dst, tree_recv.at[phase]).wait()

    def sent(phase, dst):
        pltpu.make_async_copy(dst, dst, tree_send.at[phase]).wait()

    for copy in loads[:5]:
        copy.wait()
    shape = (layers, rows, cols)
    plane_of = iota(shape, 0)
    row_of = iota(shape, 1)
    col_of = iota(shape, 2)
    links[0] = jnp.where(gx * rows + row_of < rows * sx - 1, cx_ref[...], 0.0)
    links[1] = jnp.where(gy * cols + col_of < cols * sy - 1, cy_ref[...], 0.0)
    links[2] = jnp.where(
        gl * layers + plane_of < layers * sl - 1, via_ref[...].astype(jnp.float32) * VIA_G, 0.0
    )
    lxsend[...] = links[0, :, rows - 1 : rows, :]

    tile_shape = (grid_rows, LANES)
    trow = iota(tile_shape, 0)
    tlane = iota(tile_shape, 1)
    lane0 = gl * nyc + gy * KY
    valid = tlane < sl * nyc

    def restrict_into(tile, field, shift):
        flat = jnp.sum(field, axis=0)
        for a in range(KX):
            for b in range(KY):
                val = sum_all(flat[a * br : (a + 1) * br, b * bc : (b + 1) * bc])
                here = (trow == gx * KX + a) & (tlane == lane0 + b + shift)
                tile = jnp.where(here, val, tile)
        return tile

    def send_tile(phase):
        def one(k, carry):
            pltpu.make_async_remote_copy(
                src_ref=tsend.at[phase],
                dst_ref=trecv.at[phase, k - 1],
                send_sem=tile_send.at[phase],
                recv_sem=tile_recv.at[phase],
                device_id=coords(lax.rem(me + k, n)),
                device_id_type=MESH,
            ).start()
            return carry

        lax.fori_loop(1, n, one, 0)

    def wait_tile(phase):
        every = trecv.at[phase]
        pltpu.make_async_copy(every, every, tile_recv.at[phase]).wait()
        return jnp.sum(trecv[phase], axis=0) + tsend[phase]

    def drain_tile(phase):
        every = trecv.at[phase]
        pltpu.make_async_copy(every, every, tile_send.at[phase]).wait()

    tile = jnp.zeros(tile_shape, jnp.float32)
    tile = restrict_into(tile, load_ref[...], 0)
    tsend[0] = restrict_into(tile, pad_ref[...], HALF)

    def remote(src, dst, send, recv, device):
        return pltpu.make_async_remote_copy(
            src_ref=src, dst_ref=dst, send_sem=send, recv_sem=recv,
            device_id=device, device_id_type=MESH,
        )

    last = pl.ds(cols - LANES, LANES)
    link_copies = [
        remote(lxsend, lxrecv, link_send.at[0], link_recv.at[0], up_dev[0]),
        remote(links.at[1, :, :, last], lyrecv, link_send.at[1], link_recv.at[1], up_dev[1]),
        remote(links.at[2, layers - 1], lzrecv, link_send.at[2], link_recv.at[2], up_dev[2]),
    ]

    def halo_copies(h):
        pairs = [
            (xsend.at[h, 0], xrecv.at[h, 0], up_dev[0]),
            (xsend.at[h, 1], xrecv.at[h, 1], down_dev[0]),
            (w_ref.at[h, :, :, last], yrecv.at[h, 0], up_dev[1]),
            (w_ref.at[h, :, :, pl.ds(0, LANES)], yrecv.at[h, 1], down_dev[1]),
            (w_ref.at[h, layers - 1], zrecv.at[h, 0], up_dev[2]),
            (w_ref.at[h, 0], zrecv.at[h, 1], down_dev[2]),
        ]
        return [
            remote(src, dst, halo_send.at[h, i], halo_recv.at[h, i], dev)
            for i, (src, dst, dev) in enumerate(pairs)
        ]

    def from_below(v, x_lo, y_lo, z_lo):
        vx = jnp.where(row_of == 0, x_lo, pltpu.roll(v, 1, 1))
        edge = jnp.concatenate([pltpu.roll(y_lo, 1, 2), v[:, :, LANES:]], axis=2)
        vy = jnp.where(col_of == 0, edge, pltpu.roll(v, 1, 2))
        vz = jnp.concatenate([z_lo[None], v[:-1]], axis=0)
        return vx, vy, vz

    def from_above(v, x_hi, y_hi, z_hi):
        vx = jnp.where(row_of == rows - 1, x_hi, pltpu.roll(v, rows - 1, 1))
        edge = jnp.concatenate([v[:, :, :-LANES], pltpu.roll(y_hi, LANES - 1, 2)], axis=2)
        vy = jnp.where(col_of == cols - 1, edge, pltpu.roll(v, cols - 1, 2))
        vz = jnp.concatenate([v[1:], z_hi[None]], axis=0)
        return vx, vy, vz

    pl.semaphore_wait(barrier, n - 1)
    for copy in link_copies:
        copy.start()
    send_tile(0)

    for copy in loads[5:]:
        copy.wait()
    ssend[...] = to_slots(stress_ref[...])
    exchange(0, ssend, srecv, 1)
    sort_lanes(index_ref, hi_ref, lo_ref, layers)

    for copy in link_copies:
        copy.wait()
    down_x, _, _ = from_below(links[0], lxrecv[...], lyrecv[...], lzrecv[...])
    _, down_y, _ = from_below(links[1], lxrecv[...], lyrecv[...], lzrecv[...])
    _, _, down_z = from_below(links[2], lxrecv[...], lyrecv[...], lzrecv[...])
    downs[0] = down_x
    downs[1] = down_y
    downs[2] = down_z
    diag = pad_ref[...] + links[0] + down_x + links[1] + down_y + links[2] + down_z
    dinv = OMEGA / diag
    dinv_ref[...] = dinv
    w0 = load_ref[...] * dinv

    def put_halo(h, w):
        w_ref[h] = w
        xsend[h, 0] = w[:, rows - 1 : rows, :]
        xsend[h, 1] = w[:, 0:1, :]

    put_halo(0, w0)
    first = halo_copies(0)
    for copy in first:
        copy.start()

    b1 = inverse_ref[0]
    b2 = exact(b1, b1)
    power_ref[0] = b2
    power_ref[1] = b1 + b2

    total0 = wait_tile(0)
    c0 = jnp.where(valid, total0, 0.0)
    cfull = jnp.where(valid, pltpu.roll(total0, LANES - HALF, 1), 0.0) + 6.0 * COARSE_G
    in_layer = lax.rem(tlane, nyc)

    def coarse(c):
        y = TAU * c / cfull
        for _ in range(SWEEPS - 1):
            near = jnp.where(trow > 0, pltpu.roll(y, 1, 0), 0.0)
            near += jnp.where(trow < grid_rows - 1, pltpu.roll(y, grid_rows - 1, 0), 0.0)
            near += jnp.where(in_layer > 0, pltpu.roll(y, 1, 1), 0.0)
            near += jnp.where(in_layer < nyc - 1, pltpu.roll(y, LANES - 1, 1), 0.0)
            near += jnp.where(tlane >= nyc, pltpu.roll(y, nyc, 1), 0.0)
            near += jnp.where(tlane < (sl - 1) * nyc, pltpu.roll(y, LANES - nyc, 1), 0.0)
            y = y + TAU * (c - (cfull * y - COARSE_G * near)) / cfull
            y = jnp.where(valid, y, 0.0)
        return y

    def spread(y):
        t = pltpu.roll(y, lax.rem(grid_rows + 1 - gx * KX, grid_rows), 0)
        t = pltpu.roll(t, lax.rem(LANES + 1 - lane0, LANES), 1)

        def bcast(src, r, c, height):
            return jnp.broadcast_to(src[r : r + 1, c : c + 1], (height, bc))

        def across(src, r, height):
            return jnp.concatenate([bcast(src, r, 1 + b, height) for b in range(KY)], axis=1)

        def whole(src):
            return jnp.concatenate([across(src, 1 + a, br) for a in range(KX)], axis=0)

        def side(c):
            parts = [
                jnp.broadcast_to(t[1 + a : 2 + a, c : c + 1], (br, LANES)) for a in range(KX)
            ]
            return jnp.concatenate(parts, axis=0)

        above = pltpu.roll(t, LANES - nyc, 1)
        below = pltpu.roll(t, nyc, 1)
        return (
            whole(t),
            (across(t, 0, 1), across(t, KX + 1, 1)),
            (side(0), side(KY + 1)),
            (whole(below), whole(above)),
        )

    def operate(v, lows, highs):
        bx, by, bz = from_below(v, *lows)
        ax, ay, az = from_above(v, *highs)
        out = pad_ref[...] * v
        out = out + links[0] * (v - ax) + downs[0] * (v - bx)
        out = out + links[1] * (v - ay) + downs[1] * (v - by)
        return out + links[2] * (v - az) + downs[2] * (v - bz)

    y0 = coarse(c0)
    own0, x0, yy0, z0 = spread(y0)
    coarse_dot0 = sum_all(c0 * y0)
    p0 = w0 + own0[None]
    p_ref[...] = p0
    for copy in first:
        copy.wait()

    lows0 = (xrecv[0, 0] + x0[0][None], yrecv[0, 0] + yy0[0][None], zrecv[0, 0] + z0[0])
    highs0 = (xrecv[0, 1] + x0[1][None], yrecv[0, 1] + yy0[1][None], zrecv[0, 1] + z0[1])
    q0 = operate(p0, lows0, highs0)
    wq = q0 * dinv_ref[...]
    put_halo(1, wq)
    second = halo_copies(1)
    for copy in second:
        copy.start()

    r0 = load_ref[...]
    tile = restrict_into(jnp.zeros(tile_shape, jnp.float32), q0, 0)
    sums = (sum_all(p0 * q0), sum_all(r0 * w_ref[0]), sum_all(r0 * wq), sum_all(q0 * wq))
    for i, val in enumerate(sums):
        tile = jnp.where((trow == 0) & (tlane == HALF + i), val, tile)
    tsend[1] = tile
    send_tile(1)
    b2 = power_ref[0]
    b4 = exact(b2, b2)
    power_ref[0] = b4
    power_ref[1] = power_ref[1] + exact(b2, power_ref[1])
    total1 = wait_tile(1)

    pq0, rr, rq, qq = (total1[0:1, HALF + i : HALF + i + 1] for i in range(4))
    rz0 = rr + coarse_dot0
    alpha0 = rz0 / pq0
    c1 = jnp.where(valid, c0 - alpha0 * total1, 0.0)
    y1 = coarse(c1)
    rz1 = rr - 2.0 * alpha0 * rq + alpha0 * alpha0 * qq + sum_all(c1 * y1)
    beta = rz1 / rz0
    own1, x1, yy1, z1 = spread(y1)

    p1 = w_ref[0] - alpha0 * w_ref[1] + own1[None] + beta * p_ref[...]
    for copy in second:
        copy.wait()

    def next_halo(first_w, second_w, first_y, second_y):
        return first_w - alpha0 * second_w + second_y + beta * (first_w + first_y)

    lows1, highs1 = (
        (
            next_halo(xrecv[0, s], xrecv[1, s], x0[s][None], x1[s][None]),
            next_halo(yrecv[0, s], yrecv[1, s], yy0[s][None], yy1[s][None]),
            next_halo(zrecv[0, s], zrecv[1, s], z0[s], z1[s]),
        )
        for s in range(2)
    )
    q1 = operate(p1, lows1, highs1)
    tsend[2] = jnp.where((trow == 0) & (tlane == 0), sum_all(p1 * q1), 0.0)
    send_tile(2)
    q_ref[...] = p1
    b4 = power_ref[0]
    b8 = exact(b4, b4)
    mixed = KAPPA * (power_ref[1] + exact(b4, power_ref[1]))
    power_ref[1] = exact(mixed, segment_order(segs, layers).astype(jnp.float32))
    arrived(0, srecv)
    base_ref[0:capacity] = rows_by(ssend[0], b8)
    base_ref[capacity:slots] = rows_by(srecv[...].reshape(slots - capacity, segs), b8)
    drain_tile(0)
    drain_tile(1)
    sent(0, srecv)
    total2 = wait_tile(2)
    alpha1 = rz1 / total2[0:1, 0:1]
    drop = alpha0 * p_ref[...] + alpha1 * q_ref[...]
    drop_ref[...] = drop
    flow_ref[...] = links[0] * (drop - pltpu.roll(drop, rows - 1, 1))
    current = pick(flow_ref, hi_ref, lo_ref, acc_ref)
    fsend[...] = to_slots(current)
    exchange(1, fsend, frecv, 1)
    drain_tile(2)
    arrived(1, frecv)
    gsend[0] = base_ref[0:capacity] + rows_by(fsend[0], power_ref[1])
    rest = rows_by(frecv[...].reshape(slots - capacity, segs), power_ref[1])
    rest = rest + base_ref[capacity:slots]
    gsend[1:np_] = rest.reshape(np_ - 1, capacity, segs)
    exchange(2, gsend, grecv, -1)
    sent(1, frecv)
    arrived(2, grecv)
    back = jnp.concatenate([gsend[0], grecv[...].reshape(slots - capacity, segs)], axis=0)
    final_ref[...] = exact(onehot_ref[...], back)
    sent(2, grecv)


def segment_order(segs, layers):
    per = segs // layers
    source = iota((segs, segs), 0)
    target = iota((segs, segs), 1)
    return source == (target % per) * layers + target // per


def run_all(sizes, load_current, pad_cond, cond_x, cond_y, via_map, branch_index, tree_owner, initial_stress, block_inverse):
    sx, sy, sl = sizes
    n = sx * sy * sl
    layers, rows, cols = load_current.shape
    field = (layers, rows, cols)
    f32 = jnp.float32
    vmem = pltpu.VMEM
    dma = pltpu.SemaphoreType.DMA
    i32 = jnp.int32
    trees, segs = initial_stress.shape
    capacity = -(-2 * trees // (sx * sy) // 8) * 8
    slots = sx * sy * capacity
    sent = (sx * sy, capacity, segs)
    got = (sx * sy - 1, capacity, segs)
    packed = (layers, trees // 2, LANES)
    spec = pl.BlockSpec(memory_space=pltpu.VMEM)
    far = pl.BlockSpec(memory_space=pl.ANY)
    return pl.pallas_call(
        functools.partial(cg_kernel, sizes, capacity),
        out_shape=(
            jax.ShapeDtypeStruct(field, f32), jax.ShapeDtypeStruct((trees, segs), f32)
        ),
        in_specs=[far] * 8 + [spec],
        out_specs=(spec, spec),
        scratch_shapes=[
            vmem(field, f32),
            vmem(field, f32),
            vmem(field, f32),
            vmem(field, f32),
            vmem(field, i32),
            vmem((trees, segs), i32),
            vmem((trees, segs), f32),
            vmem((1, segs, segs), f32),
            vmem(field, f32),
            vmem(packed, i32),
            vmem(packed, i32),
            vmem(packed, f32),
            vmem((trees, slots), f32),
            vmem((slots, segs), f32),
            vmem((2, segs, segs), f32),
            vmem(sent, f32),
            vmem(got, f32),
            vmem(sent, f32),
            vmem(got, f32),
            vmem(sent, f32),
            vmem(got, f32),
            vmem((3,) + field, f32),
            vmem((3,) + field, f32),
            vmem(field, f32),
            vmem((2,) + field, f32),
            vmem(field, f32),
            vmem(field, f32),
            vmem((2, 2, layers, 1, cols), f32),
            vmem((2, 2, layers, 1, cols), f32),
            vmem((2, 2, layers, rows, LANES), f32),
            vmem((2, 2, rows, cols), f32),
            vmem((layers, 1, cols), f32),
            vmem((layers, 1, cols), f32),
            vmem((layers, rows, LANES), f32),
            vmem((rows, cols), f32),
            vmem((3, KX * sx, LANES), f32),
            vmem((3, n - 1, KX * sx, LANES), f32),
            dma((3,)),
            dma((3,)),
            dma((2, 6)),
            dma((2, 6)),
            dma((3,)),
            dma((3,)),
            dma((8,)),
            dma((3,)),
            dma((3,)),
        ],
        compiler_params=pltpu.CompilerParams(
            collective_id=0, has_side_effects=True, vmem_limit_bytes=56 * 1024 * 1024
        ),
    )(
        load_current, pad_cond, cond_x, cond_y, via_map,
        branch_index, initial_stress, block_inverse, tree_owner,
    )


def sort_lanes(index_ref, hi_ref, lo_ref, layers):
    trees, segs = index_ref.shape
    per = segs // layers
    half = trees // 2
    index = index_ref[...]
    sort = segment_order(segs, layers).astype(jnp.bfloat16)
    hi = jnp.dot((index // LANES).astype(jnp.bfloat16), sort, preferred_element_type=jnp.float32)
    lo = jnp.dot((index % LANES).astype(jnp.bfloat16), sort, preferred_element_type=jnp.float32)
    hi = hi.astype(jnp.int32)
    lo = lo.astype(jnp.int32)
    left = iota((half, LANES), 1) < per

    def pack(v, l):
        base = (l // 2) * LANES
        top, low = v[:half, base : base + LANES], v[half:, base : base + LANES]
        if l % 2 == 0:
            return jnp.where(left, top, pltpu.roll(low, per, 1))
        return jnp.where(left, pltpu.roll(top, per, 1), low)

    for l in range(layers):
        hi_ref[l] = pack(hi, l)
        lo_ref[l] = pack(lo, l)


def pick(flow_ref, hi_ref, lo_ref, acc_ref):
    layers, rows, cols = flow_ref.shape
    blocks = cols // LANES
    half = hi_ref.shape[1]
    left = iota((half, LANES), 1) < LANES // 2
    for l in range(layers):
        want = hi_ref[l]
        lane = lo_ref[l]
        acc = jnp.zeros((half, LANES), jnp.float32)
        for i in range(rows - 1):
            for b in range(blocks):
                row = flow_ref[l, i : i + 1, b * LANES : (b + 1) * LANES]
                table = jnp.broadcast_to(row, (half, LANES))
                got = jnp.take_along_axis(table, lane, axis=1, mode="promise_in_bounds")
                acc = jnp.where(want == i * blocks + b, got, acc)
        acc_ref[l] = acc
    tops, lows = [], []
    for l in range(0, layers, 2):
        even, odd = acc_ref[l], acc_ref[l + 1]
        tops.append(jnp.where(left, even, pltpu.roll(odd, LANES // 2, 1)))
        lows.append(jnp.where(left, pltpu.roll(even, LANES // 2, 1), odd))
    return jnp.concatenate(
        [jnp.concatenate(tops, axis=1), jnp.concatenate(lows, axis=1)], axis=0
    )


def per_device(
    load_current,
    pad_cond,
    cond_x,
    cond_y,
    via_map,
    branch_index,
    tree_owner,
    initial_stress,
    block_inverse,
):
    size_x = lax.axis_size("gx")
    size_y = lax.axis_size("gy")
    size_l = lax.axis_size("layer")
    return run_all(
        (size_x, size_y, size_l),
        load_current,
        pad_cond,
        cond_x,
        cond_y,
        via_map,
        branch_index,
        tree_owner,
        initial_stress,
        block_inverse,
    )


def solution(mesh):
    return jax.shard_map(
        per_device,
        mesh=mesh,
        in_specs=(
            P("layer", "gx", "gy"),
            P("layer", "gx", "gy"),
            P("layer", "gx", "gy"),
            P("layer", "gx", "gy"),
            P("layer", "gx", "gy"),
            P(("gx", "gy", "layer"), None),
            P(("gx", "gy", "layer"), None),
            P(("gx", "gy", "layer"), None),
            P(("gx", "gy"), None, None),
        ),
        out_specs=(P("layer", "gx", "gy"), P(("gx", "gy", "layer"), None)),
        check_vma=False,
    )
```

```python
import functools

import jax
import jax.numpy as jnp
from jax import lax
from jax.experimental import pallas as pl
from jax.experimental.pallas import tpu as pltpu
from jax.sharding import PartitionSpec as P

KX = 2
KY = 4
SWEEPS = 4
STEPS = 8

OMEGA = 0.7
TAU = 0.6
VIA_G = 1.5
COARSE_G = 64.0
KAPPA = 2.0
LANES = 128
HALF = 64
MESH = pl.DeviceIdType.MESH


def iota(shape, dim):
    return lax.broadcasted_iota(jnp.int32, shape, dim)


def sum_all(v):
    while v.ndim > 2:
        v = jnp.sum(v, axis=0)
    return jnp.sum(jnp.sum(v, axis=0, keepdims=True), axis=1, keepdims=True)


def cg_kernel(
    sizes,
    capacity,
    load_in, pad_in, cx_in, cy_in, via_in, index_in, stress_in, inverse_in, owner_ref,
    drop_ref, final_ref,
    load_ref, pad_ref, cx_ref, cy_ref, via_ref, index_ref, stress_ref, inverse_ref,
    flow_ref, hi_ref, lo_ref, onehot_ref, base_ref, power_ref,
    ssend, srecv, fsend, frecv, gsend, grecv,
    links, downs, dinv_ref, w_ref, p_ref, q_ref,
    xsend, xrecv, yrecv, zrecv, lxsend, lxrecv, lyrecv, lzrecv,
    tsend, trecv,
    link_send, link_recv, halo_send, halo_recv, tile_send, tile_recv,
    in_sem, tree_send, tree_recv,
):
    sx, sy, sl = sizes
    n = sx * sy * sl
    layers, rows, cols = load_ref.shape
    br, bc = rows // KX, cols // KY
    nyc = KY * sy
    span = sl * KY * sy
    grid_rows = -(-sx // 8) * 8
    gx, gy, gl = lax.axis_index("gx"), lax.axis_index("gy"), lax.axis_index("layer")
    me = (gx * sy + gy) * sl + gl

    def coords(flat):
        return (flat // (sy * sl), (flat // sl) % sy, flat % sl)

    loads = [
        pltpu.make_async_copy(src, dst, in_sem.at[i])
        for i, (src, dst) in enumerate((
            (via_in, via_ref), (cx_in, cx_ref), (cy_in, cy_ref), (load_in, load_ref),
            (pad_in, pad_ref), (stress_in, stress_ref), (inverse_in, inverse_ref),
            (index_in, index_ref),
        ))
    ]
    for copy in loads:
        copy.start()
    barrier = pltpu.get_barrier_semaphore()

    def greet(k, carry):
        pl.semaphore_signal(
            barrier, inc=1, device_id=coords(lax.rem(me + k, n)), device_id_type=MESH
        )
        return carry

    lax.fori_loop(1, n, greet, 0)

    up_dev = (
        (lax.rem(gx + 1, sx), gy, gl),
        (gx, lax.rem(gy + 1, sy), gl),
        (gx, gy, lax.rem(gl + 1, sl)),
    )
    down_dev = (
        (lax.rem(gx + sx - 1, sx), gy, gl),
        (gx, lax.rem(gy + sy - 1, sy), gl),
        (gx, gy, lax.rem(gl + sl - 1, sl)),
    )

    np_ = sx * sy
    q = gx * sy + gy
    trees, segs = stress_ref.shape
    slots = np_ * capacity
    high = lax.Precision.HIGHEST

    def exact(a, b):
        return jnp.dot(a, b, preferred_element_type=jnp.float32, precision=high)

    def rows_by(a, b):
        return lax.dot_general(
            a, b, (((1,), (1,)), ((), ())), preferred_element_type=jnp.float32, precision=high
        )

    owner_rel = lax.rem(owner_ref[...] - q + np_, np_)
    hits = owner_rel == iota((LANES, trees), 0)
    ahead = iota((trees, trees), 0) < iota((trees, trees), 1)
    counts = jnp.dot(
        hits.astype(jnp.bfloat16), ahead.astype(jnp.bfloat16), preferred_element_type=jnp.float32
    )
    rank = jnp.sum(jnp.where(hits, counts, 0.0), axis=0, keepdims=True).astype(jnp.int32)
    slot = owner_rel * capacity + rank
    onehot_ref[...] = (slot == iota((slots, trees), 0)).astype(jnp.float32)

    def to_slots(v):
        return exact(onehot_ref[...], v).reshape(np_, capacity, v.shape[1])

    def peer(k):
        flat = lax.rem(q + k, np_)
        return (flat // sy, flat % sy, gl)

    def exchange(phase, src, dst, sign):
        def one(k, carry):
            pltpu.make_async_remote_copy(
                src_ref=src.at[k],
                dst_ref=dst.at[k - 1],
                send_sem=tree_send.at[phase],
                recv_sem=tree_recv.at[phase],
                device_id=peer(k if sign > 0 else np_ - k),
                device_id_type=MESH,
            ).start()
            return carry

        lax.fori_loop(1, np_, one, 0)

    def arrived(phase, dst):
        pltpu.make_async_copy(dst, dst, tree_recv.at[phase]).wait()

    def sent(phase, dst):
        pltpu.make_async_copy(dst, dst, tree_send.at[phase]).wait()

    for copy in loads[:5]:
        copy.wait()
    shape = (layers, rows, cols)
    plane_of = iota(shape, 0)
    row_of = iota(shape, 1)
    col_of = iota(shape, 2)
    links[0] = jnp.where(gx * rows + row_of < rows * sx - 1, cx_ref[...], 0.0)
    links[1] = jnp.where(gy * cols + col_of < cols * sy - 1, cy_ref[...], 0.0)
    links[2] = jnp.where(
        gl * layers + plane_of < layers * sl - 1, via_ref[...].astype(jnp.float32) * VIA_G, 0.0
    )
    lxsend[...] = links[0, :, rows - 1 : rows, :]

    tile_shape = (grid_rows, LANES)
    trow = iota(tile_shape, 0)
    tlane = iota(tile_shape, 1)
    lane0 = gl * nyc + gy * KY
    upper = tlane >= span
    place = lax.rem(tlane, span)
    valid = (tlane < KX * span) & (trow < sx)
    line = iota((1, LANES), 1)

    def restrict_into(tile, field, shift):
        flat = jnp.sum(field, axis=0)
        for a in range(KX):
            for b in range(KY):
                val = sum_all(flat[a * br : (a + 1) * br, b * bc : (b + 1) * bc])
                tile = jnp.where(line == a * span + lane0 + b + shift, val, tile)
        return tile

    def send_tile(phase):
        def one(k, carry):
            pltpu.make_async_remote_copy(
                src_ref=tsend.at[phase],
                dst_ref=trecv.at[phase, pl.ds(me, 1)],
                send_sem=tile_send.at[phase],
                recv_sem=tile_recv.at[phase],
                device_id=coords(lax.rem(me + k, n)),
                device_id_type=MESH,
            ).start()
            return carry

        lax.fori_loop(1, n, one, 0)

    def wait_tile(phase):
        every = trecv.at[phase, pl.ds(0, n - 1)]
        pltpu.make_async_copy(every, every, tile_recv.at[phase]).wait()
        group = sy * sl
        sender = iota((group, LANES), 0)
        total = jnp.zeros(tile_shape, jnp.float32)
        for g in range(sx):
            got = trecv[phase, g * group : (g + 1) * group, :]
            got = jnp.where(sender + g * group == me, tsend[phase], got)
            total = jnp.where(trow == g, jnp.sum(got, axis=0, keepdims=True), total)
        return total

    def drain_tile(phase):
        every = trecv.at[phase, pl.ds(0, n - 1)]
        pltpu.make_async_copy(every, every, tile_send.at[phase]).wait()

    tile = jnp.zeros((1, LANES), jnp.float32)
    tile = restrict_into(tile, load_ref[...], 0)
    tsend[0] = restrict_into(tile, pad_ref[...], HALF)

    def remote(src, dst, send, recv, device):
        return pltpu.make_async_remote_copy(
            src_ref=src, dst_ref=dst, send_sem=send, recv_sem=recv,
            device_id=device, device_id_type=MESH,
        )

    last = pl.ds(cols - LANES, LANES)
    link_copies = [
        remote(lxsend, lxrecv, link_send.at[0], link_recv.at[0], up_dev[0]),
        remote(links.at[1, :, :, last], lyrecv, link_send.at[1], link_recv.at[1], up_dev[1]),
        remote(links.at[2, layers - 1], lzrecv, link_send.at[2], link_recv.at[2], up_dev[2]),
    ]

    def halo_copies(h):
        pairs = [
            (xsend.at[h, 0], xrecv.at[h, 0], up_dev[0]),
            (xsend.at[h, 1], xrecv.at[h, 1], down_dev[0]),
            (w_ref.at[h, :, :, last], yrecv.at[h, 0], up_dev[1]),
            (w_ref.at[h, :, :, pl.ds(0, LANES)], yrecv.at[h, 1], down_dev[1]),
            (w_ref.at[h, layers - 1], zrecv.at[h, 0], up_dev[2]),
            (w_ref.at[h, 0], zrecv.at[h, 1], down_dev[2]),
        ]
        return [
            remote(src, dst, halo_send.at[h, i], halo_recv.at[h, i], dev)
            for i, (src, dst, dev) in enumerate(pairs)
        ]

    def from_below(v, x_lo, y_lo, z_lo):
        vx = jnp.where(row_of == 0, x_lo, pltpu.roll(v, 1, 1))
        edge = jnp.concatenate([pltpu.roll(y_lo, 1, 2), v[:, :, LANES:]], axis=2)
        vy = jnp.where(col_of == 0, edge, pltpu.roll(v, 1, 2))
        vz = jnp.concatenate([z_lo[None], v[:-1]], axis=0)
        return vx, vy, vz

    def from_above(v, x_hi, y_hi, z_hi):
        vx = jnp.where(row_of == rows - 1, x_hi, pltpu.roll(v, rows - 1, 1))
        edge = jnp.concatenate([v[:, :, :-LANES], pltpu.roll(y_hi, LANES - 1, 2)], axis=2)
        vy = jnp.where(col_of == cols - 1, edge, pltpu.roll(v, cols - 1, 2))
        vz = jnp.concatenate([v[1:], z_hi[None]], axis=0)
        return vx, vy, vz

    pl.semaphore_wait(barrier, n - 1)
    for copy in link_copies:
        copy.start()
    send_tile(0)

    for copy in loads[5:]:
        copy.wait()
    ssend[...] = to_slots(stress_ref[...])
    exchange(0, ssend, srecv, 1)
    sort_lanes(index_ref, hi_ref, lo_ref, layers)

    for copy in link_copies:
        copy.wait()
    down_x, _, _ = from_below(links[0], lxrecv[...], lyrecv[...], lzrecv[...])
    _, down_y, _ = from_below(links[1], lxrecv[...], lyrecv[...], lzrecv[...])
    _, _, down_z = from_below(links[2], lxrecv[...], lyrecv[...], lzrecv[...])
    downs[0] = down_x
    downs[1] = down_y
    downs[2] = down_z
    diag = pad_ref[...] + links[0] + down_x + links[1] + down_y + links[2] + down_z
    dinv = OMEGA / diag
    dinv_ref[...] = dinv
    w0 = load_ref[...] * dinv

    def put_halo(h, w):
        w_ref[h] = w
        xsend[h, 0] = w[:, rows - 1 : rows, :]
        xsend[h, 1] = w[:, 0:1, :]

    put_halo(0, w0)
    first = halo_copies(0)
    for copy in first:
        copy.start()

    b1 = inverse_ref[0]
    b2 = exact(b1, b1)
    power_ref[0] = b2
    power_ref[1] = b1 + b2

    total0 = wait_tile(0)
    c0 = jnp.where(valid, total0, 0.0)
    cfull = jnp.where(valid, pltpu.roll(total0, LANES - HALF, 1), 0.0) + 6.0 * COARSE_G
    in_layer = lax.rem(tlane, nyc)

    def coarse(c):
        y = TAU * c / cfull
        for _ in range(SWEEPS - 1):
            to_upper = pltpu.roll(y, span, 1)
            to_lower = pltpu.roll(y, LANES - span, 1)
            before = jnp.where(trow > 0, pltpu.roll(to_lower, 1, 0), 0.0)
            after = jnp.where(trow < sx - 1, pltpu.roll(to_upper, grid_rows - 1, 0), 0.0)
            near = jnp.where(upper, to_upper + after, to_lower + before)
            near += jnp.where(in_layer > 0, pltpu.roll(y, 1, 1), 0.0)
            near += jnp.where(in_layer < nyc - 1, pltpu.roll(y, LANES - 1, 1), 0.0)
            near += jnp.where(place >= nyc, pltpu.roll(y, nyc, 1), 0.0)
            near += jnp.where(place < (sl - 1) * nyc, pltpu.roll(y, LANES - nyc, 1), 0.0)
            y = y + TAU * (c - (cfull * y - COARSE_G * near)) / cfull
            y = jnp.where(valid, y, 0.0)
        return y

    def spread(y):
        t = pltpu.roll(y, lax.rem(grid_rows + 1 - gx, grid_rows), 0)
        t = pltpu.roll(t, lax.rem(LANES + 1 - lane0, LANES), 1)
        t2 = pltpu.roll(t, LANES - span, 1)
        order = iota(t.shape, 0)
        at = [t2[0:1], t[1:2], t2[1:2], t[2:3]]
        t = jnp.where(order == 0, at[0], jnp.where(order == 1, at[1], jnp.where(order == 2, at[2], at[3])))

        def bcast(src, r, c, height):
            return jnp.broadcast_to(src[r : r + 1, c : c + 1], (height, bc))

        def across(src, r, height):
            return jnp.concatenate([bcast(src, r, 1 + b, height) for b in range(KY)], axis=1)

        def whole(src):
            return jnp.concatenate([across(src, 1 + a, br) for a in range(KX)], axis=0)

        def side(c):
            parts = [
                jnp.broadcast_to(t[1 + a : 2 + a, c : c + 1], (br, LANES)) for a in range(KX)
            ]
            return jnp.concatenate(parts, axis=0)

        above = pltpu.roll(t, LANES - nyc, 1)
        below = pltpu.roll(t, nyc, 1)
        return (
            whole(t),
            (across(t, 0, 1), across(t, KX + 1, 1)),
            (side(0), side(KY + 1)),
            (whole(below), whole(above)),
        )

    def operate(v, lows, highs):
        bx, by, bz = from_below(v, *lows)
        ax, ay, az = from_above(v, *highs)
        out = pad_ref[...] * v
        out = out + links[0] * (v - ax) + downs[0] * (v - bx)
        out = out + links[1] * (v - ay) + downs[1] * (v - by)
        return out + links[2] * (v - az) + downs[2] * (v - bz)

    y0 = coarse(c0)
    own0, x0, yy0, z0 = spread(y0)
    coarse_dot0 = sum_all(c0 * y0)
    p0 = w0 + own0[None]
    p_ref[...] = p0
    for copy in first:
        copy.wait()

    lows0 = (xrecv[0, 0] + x0[0][None], yrecv[0, 0] + yy0[0][None], zrecv[0, 0] + z0[0])
    highs0 = (xrecv[0, 1] + x0[1][None], yrecv[0, 1] + yy0[1][None], zrecv[0, 1] + z0[1])
    q0 = operate(p0, lows0, highs0)
    wq = q0 * dinv_ref[...]
    put_halo(1, wq)
    second = halo_copies(1)
    for copy in second:
        copy.start()

    r0 = load_ref[...]
    tile = restrict_into(jnp.zeros((1, LANES), jnp.float32), q0, 0)
    sums = (sum_all(p0 * q0), sum_all(r0 * w_ref[0]), sum_all(r0 * wq), sum_all(q0 * wq))
    for i, val in enumerate(sums):
        tile = jnp.where(line == HALF + i, val, tile)
    tsend[1] = tile
    send_tile(1)
    b2 = power_ref[0]
    b4 = exact(b2, b2)
    power_ref[0] = b4
    power_ref[1] = power_ref[1] + exact(b2, power_ref[1])
    total1 = wait_tile(1)

    sum1 = jnp.sum(total1, axis=0, keepdims=True)
    pq0, rr, rq, qq = (sum1[0:1, HALF + i : HALF + i + 1] for i in range(4))
    rz0 = rr + coarse_dot0
    alpha0 = rz0 / pq0
    c1 = jnp.where(valid, c0 - alpha0 * total1, 0.0)
    y1 = coarse(c1)
    rz1 = rr - 2.0 * alpha0 * rq + alpha0 * alpha0 * qq + sum_all(c1 * y1)
    beta = rz1 / rz0
    own1, x1, yy1, z1 = spread(y1)

    p1 = w_ref[0] - alpha0 * w_ref[1] + own1[None] + beta * p_ref[...]
    for copy in second:
        copy.wait()

    def next_halo(first_w, second_w, first_y, second_y):
        return first_w - alpha0 * second_w + second_y + beta * (first_w + first_y)

    lows1, highs1 = (
        (
            next_halo(xrecv[0, s], xrecv[1, s], x0[s][None], x1[s][None]),
            next_halo(yrecv[0, s], yrecv[1, s], yy0[s][None], yy1[s][None]),
            next_halo(zrecv[0, s], zrecv[1, s], z0[s], z1[s]),
        )
        for s in range(2)
    )
    q1 = operate(p1, lows1, highs1)
    tsend[2] = jnp.where(line == 0, sum_all(p1 * q1), 0.0)
    send_tile(2)
    q_ref[...] = p1
    b4 = power_ref[0]
    b8 = exact(b4, b4)
    mixed = KAPPA * (power_ref[1] + exact(b4, power_ref[1]))
    power_ref[1] = exact(mixed, segment_order(segs, layers).astype(jnp.float32))
    arrived(0, srecv)
    base_ref[0:capacity] = rows_by(ssend[0], b8)
    base_ref[capacity:slots] = rows_by(srecv[...].reshape(slots - capacity, segs), b8)
    drain_tile(0)
    drain_tile(1)
    sent(0, srecv)
    total2 = wait_tile(2)
    alpha1 = rz1 / jnp.sum(total2, axis=0, keepdims=True)[0:1, 0:1]
    drop = alpha0 * p_ref[...] + alpha1 * q_ref[...]
    drop_ref[...] = drop
    flow_ref[...] = links[0] * (drop - pltpu.roll(drop, rows - 1, 1))
    for part in range(2):
        fsend[part] = to_slots(pick(flow_ref, hi_ref, lo_ref, part * layers // 2, layers // 2))
        exchange(1 + part, fsend.at[part], frecv.at[part], 1)
    drain_tile(2)
    wide = segs // 2
    own = base_ref[0:capacity]
    rest = base_ref[capacity:slots]
    for part in range(2):
        powers = power_ref[1, :, part * wide : (part + 1) * wide]
        own = own + rows_by(fsend[part, 0], powers)
        arrived(1 + part, frecv.at[part])
        rest = rest + rows_by(frecv[part].reshape(slots - capacity, wide), powers)
    gsend[0] = own
    gsend[1:np_] = rest.reshape(np_ - 1, capacity, segs)
    exchange(3, gsend, grecv, -1)
    sent(1, frecv.at[0])
    sent(2, frecv.at[1])
    arrived(3, grecv)
    back = jnp.concatenate([gsend[0], grecv[...].reshape(slots - capacity, segs)], axis=0)
    final_ref[...] = lax.dot_general(
        onehot_ref[...], back, (((0,), (0,)), ((), ())),
        preferred_element_type=jnp.float32, precision=high,
    )
    sent(3, grecv)


def segment_order(segs, layers):
    per = segs // layers
    source = iota((segs, segs), 0)
    target = iota((segs, segs), 1)
    return source == (target % per) * layers + target // per


def run_all(sizes, load_current, pad_cond, cond_x, cond_y, via_map, branch_index, tree_owner, initial_stress, block_inverse):
    sx, sy, sl = sizes
    n = sx * sy * sl
    layers, rows, cols = load_current.shape
    field = (layers, rows, cols)
    f32 = jnp.float32
    vmem = pltpu.VMEM
    dma = pltpu.SemaphoreType.DMA
    i32 = jnp.int32
    trees, segs = initial_stress.shape
    capacity = -(-2 * trees // (sx * sy) // 8) * 8
    slots = sx * sy * capacity
    sent = (sx * sy, capacity, segs)
    got = (sx * sy - 1, capacity, segs)
    packed = (layers, trees // 2, LANES)
    spec = pl.BlockSpec(memory_space=pltpu.VMEM)
    far = pl.BlockSpec(memory_space=pl.ANY)
    return pl.pallas_call(
        functools.partial(cg_kernel, sizes, capacity),
        out_shape=(
            jax.ShapeDtypeStruct(field, f32), jax.ShapeDtypeStruct((trees, segs), f32)
        ),
        in_specs=[far] * 8 + [spec],
        out_specs=(spec, spec),
        scratch_shapes=[
            vmem(field, f32),
            vmem(field, f32),
            vmem(field, f32),
            vmem(field, f32),
            vmem(field, i32),
            vmem((trees, segs), i32),
            vmem((trees, segs), f32),
            vmem((1, segs, segs), f32),
            vmem(field, f32),
            vmem(packed, i32),
            vmem(packed, i32),
            vmem((slots, trees), f32),
            vmem((slots, segs), f32),
            vmem((2, segs, segs), f32),
            vmem(sent, f32),
            vmem(got, f32),
            vmem((2,) + sent[:2] + (segs // 2,), f32),
            vmem((2,) + got[:2] + (segs // 2,), f32),
            vmem(sent, f32),
            vmem(got, f32),
            vmem((3,) + field, f32),
            vmem((3,) + field, f32),
            vmem(field, f32),
            vmem((2,) + field, f32),
            vmem(field, f32),
            vmem(field, f32),
            vmem((2, 2, layers, 1, cols), f32),
            vmem((2, 2, layers, 1, cols), f32),
            vmem((2, 2, layers, rows, LANES), f32),
            vmem((2, 2, rows, cols), f32),
            vmem((layers, 1, cols), f32),
            vmem((layers, 1, cols), f32),
            vmem((layers, rows, LANES), f32),
            vmem((rows, cols), f32),
            vmem((3, 1, LANES), f32),
            vmem((3, n, LANES), f32),
            dma((3,)),
            dma((3,)),
            dma((2, 6)),
            dma((2, 6)),
            dma((3,)),
            dma((3,)),
            dma((8,)),
            dma((4,)),
            dma((4,)),
        ],
        compiler_params=pltpu.CompilerParams(
            collective_id=0, has_side_effects=True, vmem_limit_bytes=56 * 1024 * 1024
        ),
    )(
        load_current, pad_cond, cond_x, cond_y, via_map,
        branch_index, initial_stress, block_inverse, tree_owner.reshape(1, trees),
    )


def sort_lanes(index_ref, hi_ref, lo_ref, layers):
    trees, segs = index_ref.shape
    per = segs // layers
    half = trees // 2
    index = index_ref[...]
    sort = segment_order(segs, layers).astype(jnp.bfloat16)
    hi = jnp.dot((index // LANES).astype(jnp.bfloat16), sort, preferred_element_type=jnp.float32)
    lo = jnp.dot((index % LANES).astype(jnp.bfloat16), sort, preferred_element_type=jnp.float32)
    hi = hi.astype(jnp.int32)
    lo = lo.astype(jnp.int32)
    left = iota((half, LANES), 1) < per

    def pack(v, l):
        base = (l // 2) * LANES
        top, low = v[:half, base : base + LANES], v[half:, base : base + LANES]
        if l % 2 == 0:
            return jnp.where(left, top, pltpu.roll(low, per, 1))
        return jnp.where(left, pltpu.roll(top, per, 1), low)

    for l in range(layers):
        hi_ref[l] = pack(hi, l)
        lo_ref[l] = pack(lo, l)


def pick(flow_ref, hi_ref, lo_ref, start, count):
    layers, rows, cols = flow_ref.shape
    blocks = cols // LANES
    half = hi_ref.shape[1]
    left = iota((half, LANES), 1) < LANES // 2
    picked = []
    for l in range(start, start + count):
        want = hi_ref[l]
        lane = lo_ref[l]
        acc = jnp.zeros((half, LANES), jnp.float32)
        for i in range(rows - 1):
            for b in range(blocks):
                row = flow_ref[l, i : i + 1, b * LANES : (b + 1) * LANES]
                table = jnp.broadcast_to(row, (half, LANES))
                got = jnp.take_along_axis(table, lane, axis=1, mode="promise_in_bounds")
                acc = jnp.where(want == i * blocks + b, got, acc)
        picked.append(acc)
    tops, lows = [], []
    for even, odd in zip(picked[0::2], picked[1::2]):
        tops.append(jnp.where(left, even, pltpu.roll(odd, LANES // 2, 1)))
        lows.append(jnp.where(left, pltpu.roll(even, LANES // 2, 1), odd))
    return jnp.concatenate(
        [jnp.concatenate(tops, axis=1), jnp.concatenate(lows, axis=1)], axis=0
    )


def per_device(
    load_current,
    pad_cond,
    cond_x,
    cond_y,
    via_map,
    branch_index,
    tree_owner,
    initial_stress,
    block_inverse,
):
    size_x = lax.axis_size("gx")
    size_y = lax.axis_size("gy")
    size_l = lax.axis_size("layer")
    return run_all(
        (size_x, size_y, size_l),
        load_current,
        pad_cond,
        cond_x,
        cond_y,
        via_map,
        branch_index,
        tree_owner,
        initial_stress,
        block_inverse,
    )


def solution(mesh):
    return jax.shard_map(
        per_device,
        mesh=mesh,
        in_specs=(
            P("layer", "gx", "gy"),
            P("layer", "gx", "gy"),
            P("layer", "gx", "gy"),
            P("layer", "gx", "gy"),
            P("layer", "gx", "gy"),
            P(("gx", "gy", "layer"), None),
            P(("gx", "gy", "layer"), None),
            P(("gx", "gy", "layer"), None),
            P(("gx", "gy"), None, None),
        ),
        out_specs=(P("layer", "gx", "gy"), P(("gx", "gy", "layer"), None)),
        check_vma=False,
    )
```

```python
import functools

import jax
import jax.numpy as jnp
from jax import lax
from jax.experimental import pallas as pl
from jax.experimental.pallas import tpu as pltpu
from jax.sharding import PartitionSpec as P

KX = 2
KY = 4
SWEEPS = 4
STEPS = 8

OMEGA = 0.7
TAU = 0.6
VIA_G = 1.5
COARSE_G = 64.0
KAPPA = 2.0
LANES = 128
HALF = 64
MESH = pl.DeviceIdType.MESH


def iota(shape, dim):
    return lax.broadcasted_iota(jnp.int32, shape, dim)


def sum_all(v):
    while v.ndim > 2:
        v = jnp.sum(v, axis=0)
    return jnp.sum(jnp.sum(v, axis=0, keepdims=True), axis=1, keepdims=True)


def cg_kernel(
    sizes,
    capacity,
    load_in, pad_in, cx_in, cy_in, via_in, index_in, stress_in, inverse_in, owner_ref,
    drop_ref, final_ref,
    load_ref, pad_ref, cx_ref, cy_ref, via_ref, index_ref, stress_ref, inverse_ref,
    flow_ref, hi_ref, lo_ref, onehot_ref, base_ref, power_ref,
    ssend, srecv, fsend, frecv, gsend, grecv,
    links, downs, dinv_ref, w_ref, p_ref, q_ref,
    xsend, xrecv, yrecv, zrecv, lxsend, lxrecv, lyrecv, lzrecv,
    tsend, trecv,
    link_send, link_recv, halo_send, halo_recv, tile_send, tile_recv,
    in_sem, tree_send, tree_recv,
):
    sx, sy, sl = sizes
    n = sx * sy * sl
    layers, rows, cols = load_ref.shape
    br, bc = rows // KX, cols // KY
    nyc = KY * sy
    span = sl * KY * sy
    grid_rows = -(-sx // 8) * 8
    gx, gy, gl = lax.axis_index("gx"), lax.axis_index("gy"), lax.axis_index("layer")
    me = (gx * sy + gy) * sl + gl

    ys = [lax.rem(gy + d, sy) for d in range(sy)]
    zs = [lax.rem(gl + d, sl) for d in range(sl)]

    def each_peer(act):
        def column(dx, carry):
            x = lax.rem(gx + dx, sx)
            for y in ys:
                for z in zs:
                    act((x, y, z))
            return carry

        if sx <= 4:
            for dx in range(1, sx):
                column(dx, 0)
        else:
            lax.fori_loop(1, sx, column, 0)
        for dy in range(sy):
            for dz in range(sl):
                if dy or dz:
                    act((gx, ys[dy], zs[dz]))

    loads = [
        pltpu.make_async_copy(src, dst, in_sem.at[i])
        for i, (src, dst) in enumerate((
            (via_in, via_ref), (cx_in, cx_ref), (cy_in, cy_ref), (load_in, load_ref),
            (pad_in, pad_ref), (stress_in, stress_ref), (inverse_in, inverse_ref),
            (index_in, index_ref),
        ))
    ]
    for copy in loads:
        copy.start()
    barrier = pltpu.get_barrier_semaphore()

    def greet(device):
        pl.semaphore_signal(barrier, inc=1, device_id=device, device_id_type=MESH)

    each_peer(greet)

    up_dev = (
        (lax.rem(gx + 1, sx), gy, gl),
        (gx, lax.rem(gy + 1, sy), gl),
        (gx, gy, lax.rem(gl + 1, sl)),
    )
    down_dev = (
        (lax.rem(gx + sx - 1, sx), gy, gl),
        (gx, lax.rem(gy + sy - 1, sy), gl),
        (gx, gy, lax.rem(gl + sl - 1, sl)),
    )

    np_ = sx * sy
    q = gx * sy + gy
    trees, segs = stress_ref.shape
    slots = np_ * capacity
    high = lax.Precision.HIGHEST

    def exact(a, b):
        return jnp.dot(a, b, preferred_element_type=jnp.float32, precision=high)

    def rows_by(a, b):
        return lax.dot_general(
            a, b, (((1,), (1,)), ((), ())), preferred_element_type=jnp.float32, precision=high
        )

    owner_rel = lax.rem(owner_ref[...] - q + np_, np_)
    hits = owner_rel == iota((LANES, trees), 0)
    ahead = iota((trees, trees), 0) < iota((trees, trees), 1)
    counts = jnp.dot(
        hits.astype(jnp.bfloat16), ahead.astype(jnp.bfloat16), preferred_element_type=jnp.float32
    )
    rank = jnp.sum(jnp.where(hits, counts, 0.0), axis=0, keepdims=True).astype(jnp.int32)
    slot = owner_rel * capacity + rank
    onehot_ref[...] = (slot == iota((slots, trees), 0)).astype(jnp.float32)

    def to_slots(v):
        return exact(onehot_ref[...], v).reshape(np_, capacity, v.shape[1])

    def peer(k):
        flat = lax.rem(q + k, np_)
        return (flat // sy, flat % sy, gl)

    def exchange(phase, src, dst, sign):
        def one(k, carry):
            pltpu.make_async_remote_copy(
                src_ref=src.at[k],
                dst_ref=dst.at[k - 1],
                send_sem=tree_send.at[phase],
                recv_sem=tree_recv.at[phase],
                device_id=peer(k if sign > 0 else np_ - k),
                device_id_type=MESH,
            ).start()
            return carry

        if np_ <= 16:
            for k in range(1, np_):
                one(k, 0)
        else:
            lax.fori_loop(1, np_, one, 0)

    def arrived(phase, dst):
        pltpu.make_async_copy(dst, dst, tree_recv.at[phase]).wait()

    def sent(phase, dst):
        pltpu.make_async_copy(dst, dst, tree_send.at[phase]).wait()

    for copy in loads[:5]:
        copy.wait()
    shape = (layers, rows, cols)
    plane_of = iota(shape, 0)
    row_of = iota(shape, 1)
    col_of = iota(shape, 2)
    links[0] = jnp.where(gx * rows + row_of < rows * sx - 1, cx_ref[...], 0.0)
    links[1] = jnp.where(gy * cols + col_of < cols * sy - 1, cy_ref[...], 0.0)
    links[2] = jnp.where(
        gl * layers + plane_of < layers * sl - 1, via_ref[...].astype(jnp.float32) * VIA_G, 0.0
    )
    lxsend[...] = links[0, :, rows - 1 : rows, :]

    tile_shape = (grid_rows, LANES)
    trow = iota(tile_shape, 0)
    tlane = iota(tile_shape, 1)
    lane0 = gl * nyc + gy * KY
    upper = tlane >= span
    place = lax.rem(tlane, span)
    valid = (tlane < KX * span) & (trow < sx)
    line = iota((1, LANES), 1)

    def restrict_into(tile, field, shift):
        flat = jnp.sum(field, axis=0)
        for a in range(KX):
            for b in range(KY):
                val = sum_all(flat[a * br : (a + 1) * br, b * bc : (b + 1) * bc])
                tile = jnp.where(line == a * span + lane0 + b + shift, val, tile)
        return tile

    def send_tile(phase):
        def one(device):
            pltpu.make_async_remote_copy(
                src_ref=tsend.at[phase],
                dst_ref=trecv.at[phase, pl.ds(me, 1)],
                send_sem=tile_send.at[phase],
                recv_sem=tile_recv.at[phase],
                device_id=device,
                device_id_type=MESH,
            ).start()

        each_peer(one)

    def wait_tile(phase):
        every = trecv.at[phase, pl.ds(0, n - 1)]
        pltpu.make_async_copy(every, every, tile_recv.at[phase]).wait()
        group = sy * sl
        sender = iota((group, LANES), 0)
        total = jnp.zeros(tile_shape, jnp.float32)
        for g in range(sx):
            got = trecv[phase, g * group : (g + 1) * group, :]
            got = jnp.where(sender + g * group == me, tsend[phase], got)
            total = jnp.where(trow == g, jnp.sum(got, axis=0, keepdims=True), total)
        return total

    def drain_tile(phase):
        every = trecv.at[phase, pl.ds(0, n - 1)]
        pltpu.make_async_copy(every, every, tile_send.at[phase]).wait()

    tile = jnp.zeros((1, LANES), jnp.float32)
    tile = restrict_into(tile, load_ref[...], 0)
    tsend[0] = restrict_into(tile, pad_ref[...], HALF)

    def remote(src, dst, send, recv, device):
        return pltpu.make_async_remote_copy(
            src_ref=src, dst_ref=dst, send_sem=send, recv_sem=recv,
            device_id=device, device_id_type=MESH,
        )

    last = pl.ds(cols - LANES, LANES)
    link_copies = [
        remote(lxsend, lxrecv, link_send.at[0], link_recv.at[0], up_dev[0]),
        remote(links.at[1, :, :, last], lyrecv, link_send.at[1], link_recv.at[1], up_dev[1]),
        remote(links.at[2, layers - 1], lzrecv, link_send.at[2], link_recv.at[2], up_dev[2]),
    ]

    def halo_copies(h):
        pairs = [
            (xsend.at[h, 0], xrecv.at[h, 0], up_dev[0]),
            (xsend.at[h, 1], xrecv.at[h, 1], down_dev[0]),
            (w_ref.at[h, :, :, last], yrecv.at[h, 0], up_dev[1]),
            (w_ref.at[h, :, :, pl.ds(0, LANES)], yrecv.at[h, 1], down_dev[1]),
            (w_ref.at[h, layers - 1], zrecv.at[h, 0], up_dev[2]),
            (w_ref.at[h, 0], zrecv.at[h, 1], down_dev[2]),
        ]
        return [
            remote(src, dst, halo_send.at[h, i], halo_recv.at[h, i], dev)
            for i, (src, dst, dev) in enumerate(pairs)
        ]

    def from_below(v, x_lo, y_lo, z_lo):
        vx = jnp.where(row_of == 0, x_lo, pltpu.roll(v, 1, 1))
        edge = jnp.concatenate([pltpu.roll(y_lo, 1, 2), v[:, :, LANES:]], axis=2)
        vy = jnp.where(col_of == 0, edge, pltpu.roll(v, 1, 2))
        vz = jnp.concatenate([z_lo[None], v[:-1]], axis=0)
        return vx, vy, vz

    def from_above(v, x_hi, y_hi, z_hi):
        vx = jnp.where(row_of == rows - 1, x_hi, pltpu.roll(v, rows - 1, 1))
        edge = jnp.concatenate([v[:, :, :-LANES], pltpu.roll(y_hi, LANES - 1, 2)], axis=2)
        vy = jnp.where(col_of == cols - 1, edge, pltpu.roll(v, cols - 1, 2))
        vz = jnp.concatenate([v[1:], z_hi[None]], axis=0)
        return vx, vy, vz

    for copy in loads[5:]:
        copy.wait()
    ssend[...] = to_slots(stress_ref[...])
    sort_lanes(index_ref, hi_ref, lo_ref, layers)
    b1 = inverse_ref[0]
    b2 = exact(b1, b1)
    power_ref[0] = b2
    power_ref[1] = b1 + b2
    pl.semaphore_wait(barrier, n - 1)
    for copy in link_copies:
        copy.start()
    send_tile(0)


    for copy in link_copies:
        copy.wait()
    down_x, _, _ = from_below(links[0], lxrecv[...], lyrecv[...], lzrecv[...])
    _, down_y, _ = from_below(links[1], lxrecv[...], lyrecv[...], lzrecv[...])
    _, _, down_z = from_below(links[2], lxrecv[...], lyrecv[...], lzrecv[...])
    downs[0] = down_x
    downs[1] = down_y
    downs[2] = down_z
    diag = pad_ref[...] + links[0] + down_x + links[1] + down_y + links[2] + down_z
    dinv = OMEGA / diag
    dinv_ref[...] = dinv
    w0 = load_ref[...] * dinv

    def put_halo(h, w):
        w_ref[h] = w
        xsend[h, 0] = w[:, rows - 1 : rows, :]
        xsend[h, 1] = w[:, 0:1, :]

    put_halo(0, w0)
    first = halo_copies(0)
    for copy in first:
        copy.start()
    exchange(0, ssend, srecv, 1)


    total0 = wait_tile(0)
    c0 = jnp.where(valid, total0, 0.0)
    cfull = jnp.where(valid, pltpu.roll(total0, LANES - HALF, 1), 0.0) + 6.0 * COARSE_G
    in_layer = lax.rem(tlane, nyc)

    def coarse(c):
        y = TAU * c / cfull
        for _ in range(SWEEPS - 1):
            to_upper = pltpu.roll(y, span, 1)
            to_lower = pltpu.roll(y, LANES - span, 1)
            before = jnp.where(trow > 0, pltpu.roll(to_lower, 1, 0), 0.0)
            after = jnp.where(trow < sx - 1, pltpu.roll(to_upper, grid_rows - 1, 0), 0.0)
            near = jnp.where(upper, to_upper + after, to_lower + before)
            near += jnp.where(in_layer > 0, pltpu.roll(y, 1, 1), 0.0)
            near += jnp.where(in_layer < nyc - 1, pltpu.roll(y, LANES - 1, 1), 0.0)
            near += jnp.where(place >= nyc, pltpu.roll(y, nyc, 1), 0.0)
            near += jnp.where(place < (sl - 1) * nyc, pltpu.roll(y, LANES - nyc, 1), 0.0)
            y = y + TAU * (c - (cfull * y - COARSE_G * near)) / cfull
            y = jnp.where(valid, y, 0.0)
        return y

    def spread(y):
        t = pltpu.roll(y, lax.rem(grid_rows + 1 - gx, grid_rows), 0)
        t = pltpu.roll(t, lax.rem(LANES + 1 - lane0, LANES), 1)
        t2 = pltpu.roll(t, LANES - span, 1)
        order = iota(t.shape, 0)
        at = [t2[0:1], t[1:2], t2[1:2], t[2:3]]
        t = jnp.where(order == 0, at[0], jnp.where(order == 1, at[1], jnp.where(order == 2, at[2], at[3])))

        def bcast(src, r, c, height):
            return jnp.broadcast_to(src[r : r + 1, c : c + 1], (height, bc))

        def across(src, r, height):
            return jnp.concatenate([bcast(src, r, 1 + b, height) for b in range(KY)], axis=1)

        def whole(src):
            return jnp.concatenate([across(src, 1 + a, br) for a in range(KX)], axis=0)

        def side(c):
            parts = [
                jnp.broadcast_to(t[1 + a : 2 + a, c : c + 1], (br, LANES)) for a in range(KX)
            ]
            return jnp.concatenate(parts, axis=0)

        above = pltpu.roll(t, LANES - nyc, 1)
        below = pltpu.roll(t, nyc, 1)
        return (
            whole(t),
            (across(t, 0, 1), across(t, KX + 1, 1)),
            (side(0), side(KY + 1)),
            (whole(below), whole(above)),
        )

    def operate(v, lows, highs):
        bx, by, bz = from_below(v, *lows)
        ax, ay, az = from_above(v, *highs)
        out = pad_ref[...] * v
        out = out + links[0] * (v - ax) + downs[0] * (v - bx)
        out = out + links[1] * (v - ay) + downs[1] * (v - by)
        return out + links[2] * (v - az) + downs[2] * (v - bz)

    y0 = coarse(c0)
    own0, x0, yy0, z0 = spread(y0)
    coarse_dot0 = sum_all(c0 * y0)
    p0 = w0 + own0[None]
    p_ref[...] = p0
    for copy in first:
        copy.wait()

    lows0 = (xrecv[0, 0] + x0[0][None], yrecv[0, 0] + yy0[0][None], zrecv[0, 0] + z0[0])
    highs0 = (xrecv[0, 1] + x0[1][None], yrecv[0, 1] + yy0[1][None], zrecv[0, 1] + z0[1])
    q0 = operate(p0, lows0, highs0)
    wq = q0 * dinv_ref[...]
    put_halo(1, wq)
    second = halo_copies(1)
    for copy in second:
        copy.start()

    r0 = load_ref[...]
    tile = restrict_into(jnp.zeros((1, LANES), jnp.float32), q0, 0)
    sums = (sum_all(p0 * q0), sum_all(r0 * w_ref[0]), sum_all(r0 * wq), sum_all(q0 * wq))
    for i, val in enumerate(sums):
        tile = jnp.where(line == HALF + i, val, tile)
    tsend[1] = tile
    send_tile(1)
    b2 = power_ref[0]
    b4 = exact(b2, b2)
    power_ref[0] = b4
    power_ref[1] = power_ref[1] + exact(b2, power_ref[1])
    total1 = wait_tile(1)

    sum1 = jnp.sum(total1, axis=0, keepdims=True)
    pq0, rr, rq, qq = (sum1[0:1, HALF + i : HALF + i + 1] for i in range(4))
    rz0 = rr + coarse_dot0
    alpha0 = rz0 / pq0
    c1 = jnp.where(valid, c0 - alpha0 * total1, 0.0)
    y1 = coarse(c1)
    rz1 = rr - 2.0 * alpha0 * rq + alpha0 * alpha0 * qq + sum_all(c1 * y1)
    beta = rz1 / rz0
    own1, x1, yy1, z1 = spread(y1)

    p1 = w_ref[0] - alpha0 * w_ref[1] + own1[None] + beta * p_ref[...]
    for copy in second:
        copy.wait()

    def next_halo(first_w, second_w, first_y, second_y):
        return first_w - alpha0 * second_w + second_y + beta * (first_w + first_y)

    lows1, highs1 = (
        (
            next_halo(xrecv[0, s], xrecv[1, s], x0[s][None], x1[s][None]),
            next_halo(yrecv[0, s], yrecv[1, s], yy0[s][None], yy1[s][None]),
            next_halo(zrecv[0, s], zrecv[1, s], z0[s], z1[s]),
        )
        for s in range(2)
    )
    q1 = operate(p1, lows1, highs1)
    tsend[2] = jnp.where(line == 0, sum_all(p1 * q1), 0.0)
    send_tile(2)
    q_ref[...] = p1
    b4 = power_ref[0]
    b8 = exact(b4, b4)
    mixed = KAPPA * (power_ref[1] + exact(b4, power_ref[1]))
    power_ref[1] = exact(mixed, segment_order(segs, layers).astype(jnp.float32))
    arrived(0, srecv)
    base_ref[0:capacity] = rows_by(ssend[0], b8)
    base_ref[capacity:slots] = rows_by(srecv[...].reshape(slots - capacity, segs), b8)
    drain_tile(0)
    drain_tile(1)
    sent(0, srecv)
    total2 = wait_tile(2)
    alpha1 = rz1 / jnp.sum(total2, axis=0, keepdims=True)[0:1, 0:1]
    drop = alpha0 * p_ref[...] + alpha1 * q_ref[...]
    drop_ref[...] = drop
    flow_ref[...] = links[0] * (drop - pltpu.roll(drop, rows - 1, 1))
    for part in range(2):
        fsend[part] = to_slots(pick(flow_ref, hi_ref, lo_ref, part * layers // 2, layers // 2))
        exchange(1 + part, fsend.at[part], frecv.at[part], 1)
    drain_tile(2)
    wide = segs // 2
    own = base_ref[0:capacity]
    rest = base_ref[capacity:slots]
    for part in range(2):
        powers = power_ref[1, :, part * wide : (part + 1) * wide]
        own = own + rows_by(fsend[part, 0], powers)
        arrived(1 + part, frecv.at[part])
        rest = rest + rows_by(frecv[part].reshape(slots - capacity, wide), powers)
    gsend[0] = own
    gsend[1:np_] = rest.reshape(np_ - 1, capacity, segs)
    exchange(3, gsend, grecv, -1)
    sent(1, frecv.at[0])
    sent(2, frecv.at[1])
    arrived(3, grecv)
    back = jnp.concatenate([gsend[0], grecv[...].reshape(slots - capacity, segs)], axis=0)
    final_ref[...] = lax.dot_general(
        onehot_ref[...], back, (((0,), (0,)), ((), ())),
        preferred_element_type=jnp.float32, precision=high,
    )
    sent(3, grecv)


def segment_order(segs, layers):
    per = segs // layers
    source = iota((segs, segs), 0)
    target = iota((segs, segs), 1)
    return source == (target % per) * layers + target // per


def run_all(sizes, load_current, pad_cond, cond_x, cond_y, via_map, branch_index, tree_owner, initial_stress, block_inverse):
    sx, sy, sl = sizes
    n = sx * sy * sl
    layers, rows, cols = load_current.shape
    field = (layers, rows, cols)
    f32 = jnp.float32
    vmem = pltpu.VMEM
    dma = pltpu.SemaphoreType.DMA
    i32 = jnp.int32
    trees, segs = initial_stress.shape
    capacity = -(-2 * trees // (sx * sy) // 8) * 8
    slots = sx * sy * capacity
    sent = (sx * sy, capacity, segs)
    got = (sx * sy - 1, capacity, segs)
    packed = (layers, trees // 2, LANES)
    spec = pl.BlockSpec(memory_space=pltpu.VMEM)
    far = pl.BlockSpec(memory_space=pl.ANY)
    return pl.pallas_call(
        functools.partial(cg_kernel, sizes, capacity),
        out_shape=(
            jax.ShapeDtypeStruct(field, f32), jax.ShapeDtypeStruct((trees, segs), f32)
        ),
        in_specs=[far] * 8 + [spec],
        out_specs=(spec, spec),
        scratch_shapes=[
            vmem(field, f32),
            vmem(field, f32),
            vmem(field, f32),
            vmem(field, f32),
            vmem(field, i32),
            vmem((trees, segs), i32),
            vmem((trees, segs), f32),
            vmem((1, segs, segs), f32),
            vmem(field, f32),
            vmem(packed, i32),
            vmem(packed, i32),
            vmem((slots, trees), f32),
            vmem((slots, segs), f32),
            vmem((2, segs, segs), f32),
            vmem(sent, f32),
            vmem(got, f32),
            vmem((2,) + sent[:2] + (segs // 2,), f32),
            vmem((2,) + got[:2] + (segs // 2,), f32),
            vmem(sent, f32),
            vmem(got, f32),
            vmem((3,) + field, f32),
            vmem((3,) + field, f32),
            vmem(field, f32),
            vmem((2,) + field, f32),
            vmem(field, f32),
            vmem(field, f32),
            vmem((2, 2, layers, 1, cols), f32),
            vmem((2, 2, layers, 1, cols), f32),
            vmem((2, 2, layers, rows, LANES), f32),
            vmem((2, 2, rows, cols), f32),
            vmem((layers, 1, cols), f32),
            vmem((layers, 1, cols), f32),
            vmem((layers, rows, LANES), f32),
            vmem((rows, cols), f32),
            vmem((3, 1, LANES), f32),
            vmem((3, n, LANES), f32),
            dma((3,)),
            dma((3,)),
            dma((2, 6)),
            dma((2, 6)),
            dma((3,)),
            dma((3,)),
            dma((8,)),
            dma((4,)),
            dma((4,)),
        ],
        compiler_params=pltpu.CompilerParams(
            collective_id=0, has_side_effects=True, vmem_limit_bytes=56 * 1024 * 1024
        ),
    )(
        load_current, pad_cond, cond_x, cond_y, via_map,
        branch_index, initial_stress, block_inverse, tree_owner.reshape(1, trees),
    )


def sort_lanes(index_ref, hi_ref, lo_ref, layers):
    trees, segs = index_ref.shape
    per = segs // layers
    half = trees // 2
    index = index_ref[...]
    sort = segment_order(segs, layers).astype(jnp.bfloat16)
    hi = jnp.dot((index // LANES).astype(jnp.bfloat16), sort, preferred_element_type=jnp.float32)
    lo = jnp.dot((index % LANES).astype(jnp.bfloat16), sort, preferred_element_type=jnp.float32)
    hi = hi.astype(jnp.int32)
    lo = lo.astype(jnp.int32)
    left = iota((half, LANES), 1) < per

    def pack(v, l):
        base = (l // 2) * LANES
        top, low = v[:half, base : base + LANES], v[half:, base : base + LANES]
        if l % 2 == 0:
            return jnp.where(left, top, pltpu.roll(low, per, 1))
        return jnp.where(left, pltpu.roll(top, per, 1), low)

    for l in range(layers):
        hi_ref[l] = pack(hi, l)
        lo_ref[l] = pack(lo, l)


def pick(flow_ref, hi_ref, lo_ref, start, count):
    layers, rows, cols = flow_ref.shape
    blocks = cols // LANES
    half = hi_ref.shape[1]
    left = iota((half, LANES), 1) < LANES // 2
    picked = []
    for l in range(start, start + count):
        want = hi_ref[l]
        lane = lo_ref[l]
        acc = jnp.zeros((half, LANES), jnp.float32)
        for i in range(rows - 1):
            for b in range(blocks):
                row = flow_ref[l, i : i + 1, b * LANES : (b + 1) * LANES]
                table = jnp.broadcast_to(row, (half, LANES))
                got = jnp.take_along_axis(table, lane, axis=1, mode="promise_in_bounds")
                acc = jnp.where(want == i * blocks + b, got, acc)
        picked.append(acc)
    tops, lows = [], []
    for even, odd in zip(picked[0::2], picked[1::2]):
        tops.append(jnp.where(left, even, pltpu.roll(odd, LANES // 2, 1)))
        lows.append(jnp.where(left, pltpu.roll(even, LANES // 2, 1), odd))
    return jnp.concatenate(
        [jnp.concatenate(tops, axis=1), jnp.concatenate(lows, axis=1)], axis=0
    )


def per_device(
    load_current,
    pad_cond,
    cond_x,
    cond_y,
    via_map,
    branch_index,
    tree_owner,
    initial_stress,
    block_inverse,
):
    size_x = lax.axis_size("gx")
    size_y = lax.axis_size("gy")
    size_l = lax.axis_size("layer")
    return run_all(
        (size_x, size_y, size_l),
        load_current,
        pad_cond,
        cond_x,
        cond_y,
        via_map,
        branch_index,
        tree_owner,
        initial_stress,
        block_inverse,
    )


def solution(mesh):
    return jax.shard_map(
        per_device,
        mesh=mesh,
        in_specs=(
            P("layer", "gx", "gy"),
            P("layer", "gx", "gy"),
            P("layer", "gx", "gy"),
            P("layer", "gx", "gy"),
            P("layer", "gx", "gy"),
            P(("gx", "gy", "layer"), None),
            P(("gx", "gy", "layer"), None),
            P(("gx", "gy", "layer"), None),
            P(("gx", "gy"), None, None),
        ),
        out_specs=(P("layer", "gx", "gy"), P(("gx", "gy", "layer"), None)),
        check_vma=False,
    )
```
